32 devices in a mesh: tm: 8 (over y, x, core), panel: 4 (over z).
Axes of the slice: x: 2, y: 2, z: 4, core: 2. Of those that a mesh axis runs over, the one named last changes fastest.
Arguments:
- transitions: float32 [32, 512, 512], P('tm', 'panel'), may hold values from -1 to 1.1, as said below
- offsets: float32 [32, 512], P('tm', 'panel'), may hold values from -1.2 to 1.2
- noise_cov: float32 [32, 512, 512], P('tm', 'panel'), may hold values from -0.05 to 0.2, as said below
Outputs:
- smoothed_means: float32 [32, 512], P('tm', 'panel')
- smoothed_covs: float32 [32, 512, 512], P('tm', 'panel')
The draws below stay inside these ranges and needn't reach their ends.
Inputs may be any that keep to these rules, and one draw needn't show every extreme that they name: `transitions`: each row is a rate times a row of a near-identity matrix. `noise_cov`: symmetric.
All inputs are finite; a program needn't handle non-finite values.
Results may differ from the reference program's by a relative error of at most 0.00027.
Values sent between devices are 32-bit elements; how exact they have to be, the bound alone decides.
A program may use at most 128 MiB of HBM per device.

```python
import math
import jax
import jax.numpy as jnp
from jax import lax

D = 512
EPOCH_COUNT_ALL = 32


def draw_transitions(key, part):
    key = jax.random.fold_in(key, 1)
    stochastic_seed_list = jax.random.split(key, 5)
    share = 0.5
    slow = jax.random.bernoulli(stochastic_seed_list[0], share, (D,))
    slow_rate = jax.random.uniform(stochastic_seed_list[1], (EPOCH_COUNT_ALL, D), jnp.float32, 0.975, 0.995)
    fast_rate = jax.random.uniform(stochastic_seed_list[2], (EPOCH_COUNT_ALL, D), jnp.float32, 0.3, 0.9)
    mean_wander_speeds = jnp.where(slow[None, :], slow_rate, fast_rate)
    draw_batch_group = jax.random.bernoulli(stochastic_seed_list[3], 4.0 / EPOCH_COUNT_ALL, (EPOCH_COUNT_ALL, 1))
    mean_wander_speeds = mean_wander_speeds * jnp.where(draw_batch_group, 0.6, 1.0)
    noise = jax.random.truncated_normal(stochastic_seed_list[4], -4.0, 4.0, (EPOCH_COUNT_ALL, D, D), jnp.float32)
    eye = jnp.eye(D, dtype=jnp.float32)
    return mean_wander_speeds[:, :, None] * (0.97 * eye[None] + 0.2 / math.sqrt(D) * noise)


def draw_noise_cov(key, part):
    key = jax.random.fold_in(key, 2)
    stochastic_seed_list = jax.random.split(key, 2)
    lower, upper = (0.005, 0.05)
    level = jax.random.uniform(stochastic_seed_list[0], (EPOCH_COUNT_ALL, D), jnp.float32, math.log(lower), math.log(upper))
    noise = jax.random.truncated_normal(stochastic_seed_list[1], -4.0, 4.0, (EPOCH_COUNT_ALL, D, D), jnp.float32)
    sym = (noise + jnp.swapaxes(noise, 1, 2)) * 0.003
    eye = jnp.eye(D, dtype=jnp.float32)
    return sym * (1.0 - eye[None]) + jnp.exp(level)[:, :, None] * eye[None]


def block_levels(key, dims, pieces, low, high):
    factor_of, own = 1.0, jax.random.fold_in(key, 6)
    for dim, shards_of in pieces:
        steps = jnp.exp(jax.random.uniform(jax.random.fold_in(own, dim), (shards_of,), jnp.float32, low / len(pieces), high / len(pieces)))
        factor_of = factor_of * jnp.repeat(steps, dims[dim] // shards_of).reshape([-1 if axis == dim else 1 for axis in range(len(dims))])
    return factor_of


def gaussian(stream_key, shape, spread, bound, shards=(), kind=jnp.bfloat16):
    values = jax.random.normal(stream_key, shape, jnp.float32) * spread
    if len(shards) > 0:
        values = block_levels(stream_key, shape, shards, -0.22, 0.18) * values
    return jnp.clip(values, min=-bound, max=bound).astype(kind)


def setup_inputs(seed: int = 0) -> dict:
    splits = jax.random.split(jax.random.key(seed), 4)
    transitions = draw_transitions(jax.random.fold_in(splits[3], 71), 0)
    offsets = gaussian(splits[1], (EPOCH_COUNT_ALL, D), 0.2, 1.2, ((0, 8), (1, 4)), jnp.float32)
    noise_cov = draw_noise_cov(jax.random.fold_in(splits[3], 71), 0)
    return dict(transitions=transitions, offsets=offsets, noise_cov=noise_cov)


def product(left, right):
    return jnp.dot(left, right, precision=lax.Precision.HIGHEST, preferred_element_type=jnp.float32)


def reference(transitions, offsets, noise_cov):
    def step(carry, items):
        mean_next, cov_next = carry
        gain, offset, cov_term = items
        mean_now = product(gain, mean_next) + offset
        cov_now = product(product(gain, cov_next), gain.T) + cov_term
        return (mean_now, cov_now), (mean_now, cov_now)

    start = (jnp.zeros((D,), jnp.float32), jnp.zeros((D, D), jnp.float32))
    _, (means, covs) = lax.scan(step, start, (transitions, offsets, noise_cov), reverse=True)
    return means, covs
```

```python
import jax
import jax.numpy as jnp
from jax import lax
from jax.sharding import PartitionSpec as P


def product(left, right):
    return jnp.dot(left, right, precision=lax.Precision.HIGH, preferred_element_type=jnp.float32)


def product_t(left, right):
    return lax.dot_general(
        left, right, (((1,), (1,)), ((), ())),
        precision=lax.Precision.HIGH, preferred_element_type=jnp.float32,
    )


def matvec(matrix, vector):
    return jnp.sum(matrix * vector[None, :], axis=1)


def send(value, pairs):
    return lax.ppermute(value, "tm", pairs)


def spread(value, core, distance, blocks, groups):
    half = value.shape[0] // 2
    own = jnp.where(core == 0, value[:half], value[half:])
    got = None
    for pair in range(distance // 2):
        pairs = [
            (base + distance + c, base + 2 * pair + c) for base in groups for c in range(2)
        ]
        part = send(own, pairs)
        got = part if got is None else got + part
    other = send(got, [(t, t ^ 1) for t in range(blocks)])
    return jnp.where(
        core == 0, jnp.concatenate([got, other]), jnp.concatenate([other, got])
    )


def later_state(gains, offsets, covs):
    blocks = lax.axis_size("tm")
    me = lax.axis_index("tm")
    core = me % 2
    swap = [(t, t ^ 1) for t in range(blocks)]
    r_gain, r_offset, r_cov = send(gains, swap), send(offsets, swap), send(covs, swap)
    lower = core == 0
    eye = jnp.eye(gains.shape[0], dtype=jnp.float32)
    x_gain = jnp.where(lower, r_gain, eye)
    x_offset = jnp.where(lower, r_offset, 0.0)
    x_cov = jnp.where(lower, r_cov, 0.0)
    first = jnp.where(lower, gains, r_gain)
    g_offset = matvec(first, jnp.where(lower, r_offset, offsets)) + jnp.where(
        lower, offsets, r_offset
    )
    g_cov = product_t(product(first, jnp.where(lower, r_cov, covs)), first) + jnp.where(
        lower, covs, r_cov
    )
    g_gain = product(first, jnp.where(lower, r_gain, gains))
    distance = 2
    while distance < blocks:
        last = 2 * distance == blocks
        groups = list(range(0, blocks, 2 * distance))
        r_cov = spread(g_cov, core, distance, blocks, groups)
        r_offset = spread(g_offset, core, distance, blocks, groups)
        lower = (me // distance) % 2 == 0
        new_cov = product_t(product(x_gain, r_cov), x_gain) + x_cov
        new_offset = matvec(x_gain, r_offset) + x_offset
        if not last:
            r_gain = spread(g_gain, core, distance, blocks, groups[:-1])
            g_offset = matvec(g_gain, r_offset) + g_offset
            g_cov = product_t(product(g_gain, r_cov), g_gain) + g_cov
            g_gain = product(g_gain, r_gain)
            x_gain = jnp.where(lower, product(x_gain, r_gain), x_gain)
        x_cov = jnp.where(lower, new_cov, x_cov)
        x_offset = jnp.where(lower, new_offset, x_offset)
        distance *= 2
    return x_offset, x_cov


def per_device(transitions, offsets, noise_cov):
    steps, rows = transitions.shape[:2]
    start = lax.axis_index("panel") * rows
    whole = {}
    for k in [*range(steps - 2, -1, -1), steps - 1]:
        whole[k] = lax.all_gather(transitions[k], "panel", axis=0, tiled=True)
    all_offsets = lax.all_gather(offsets, "panel", axis=1, tiled=True)
    cov = noise_cov[steps - 1]
    offset = all_offsets[steps - 1]
    gain = whole[steps - 1]
    covs, gains, means = [cov], [gain], [offset]
    for k in range(steps - 2, -1, -1):
        columns = product_t(whole[k], cov)
        mine = lax.all_to_all(columns, "panel", split_axis=0, concat_axis=1, tiled=True)
        cov = product_t(mine, whole[k]) + noise_cov[k]
        gain = product(whole[k], gain)
        offset = matvec(whole[k], offset) + all_offsets[k]
        covs.append(cov)
        gains.append(gain)
        means.append(offset)
    whole_cov = lax.all_gather(cov, "panel", axis=0, tiled=True)
    next_mean, next_cov = later_state(gain, offset, whole_cov)
    covs, gains, means = covs[::-1], gains[::-1], means[::-1]
    own = jnp.concatenate([lax.dynamic_slice_in_dim(f, start, rows, 0) for f in gains])
    own_offsets = jnp.concatenate(
        [lax.dynamic_slice_in_dim(m, start, rows, 0) for m in means]
    )
    mean = (matvec(own, next_mean) + own_offsets).reshape(steps, rows)
    left = product(own, next_cov).reshape(steps, rows, -1)
    out = jnp.stack([product_t(left[k], gains[k]) + covs[k] for k in range(steps)])
    return mean, out


def solution(mesh):
    placed = (P("tm", "panel", None), P("tm", "panel"), P("tm", "panel", None))
    return jax.shard_map(
        per_device,
        mesh=mesh,
        in_specs=placed,
        out_specs=(P("tm", "panel"), P("tm", "panel", None)),
        check_vma=False,
    )
```

```python
import functools

import jax
import jax.numpy as jnp
from jax import lax
from jax.experimental import pallas as pl
from jax.experimental.pallas import tpu as pltpu
from jax.sharding import PartitionSpec as P


def product(left, right):
    return jnp.dot(left, right, precision=lax.Precision.HIGH, preferred_element_type=jnp.float32)


def product_t(left, right):
    return lax.dot_general(
        left, right, (((1,), (1,)), ((), ())),
        precision=lax.Precision.HIGH, preferred_element_type=jnp.float32,
    )


def matvec(matrix, vector):
    return jnp.sum(matrix * vector[None, :], axis=1)


def halves(value):
    high = value.astype(jnp.bfloat16)
    return high, (value - high.astype(jnp.float32)).astype(jnp.bfloat16)


def three_pass(left, right, across):
    dims = (((1,), (across,)), ((), ()))
    left_high, left_low = halves(left)
    right_high, right_low = halves(right)

    def dot(a, b):
        return lax.dot_general(a, b, dims, preferred_element_type=jnp.float32)

    return dot(left_high, right_high) + (dot(left_high, right_low) + dot(left_low, right_high))


def send_order(steps, hops):
    order, reached, at = [], [0] * steps, [-2] * steps
    while len(order) < steps * hops:
        ready = [k for k in range(steps) if reached[k] < hops]
        k = next((k for k in ready if at[k] <= len(order) - 2), ready[0])
        order.append((k, reached[k]))
        reached[k] += 1
        at[k] = len(order) - 1
    return order


def block_kernel(
    n, e_ref, g_ref, l_ref, whole_ref, gains_ref, covs_ref, cov_ref, offsets_ref,
    columns_ref, pieces_ref, e_send, e_recv, z_send, z_recv, c_send, c_recv, g_send, g_recv,
):
    steps, rows, width = e_ref.shape
    me = lax.axis_index("panel")
    right = lax.rem(me + 1, n)
    peers = [lax.rem(me + d, n) for d in range(1, n)]

    def part(owner):
        return pl.ds(pl.multiple_of(owner * rows, rows), rows)

    def copy(source, target, send_sem, recv_sem, peer):
        return pltpu.make_async_remote_copy(
            src_ref=source, dst_ref=target, send_sem=send_sem, recv_sem=recv_sem,
            device_id={"panel": peer}, device_id_type=pl.DeviceIdType.MESH,
        )

    barrier = pltpu.get_barrier_semaphore()
    for peer in peers:
        pl.semaphore_signal(
            barrier, inc=1, device_id={"panel": peer}, device_id_type=pl.DeviceIdType.MESH
        )
    pl.semaphore_wait(barrier, n - 1)

    arrival = [steps - 2, steps - 1, *range(steps - 3, -1, -1)]
    order = [(arrival[k], hop) for k, hop in send_order(steps, n - 1)]
    ring, landed, sent = {}, set(), []

    def land(k, hop):
        if (k, hop) not in landed:
            ring[k, hop].wait_recv()
            landed.add((k, hop))

    def pump(count):
        for _ in range(min(count, len(order) - len(ring))):
            k, hop = order[len(ring)]
            owner = lax.rem(me - hop + n, n)
            if hop > 0:
                land(k, hop - 1)
            source = e_ref.at[k] if hop == 0 else whole_ref.at[k, part(owner)]
            ring[k, hop] = copy(
                source, whole_ref.at[k, part(owner)], e_send.at[k, hop], e_recv.at[k, hop], right
            )
            ring[k, hop].start()

    def complete(k):
        while (k, n - 2) not in ring:
            pump(1)
        land(k, n - 2)

    pump(2)
    for d, peer in enumerate(peers):
        small = copy(g_ref, offsets_ref.at[me], g_send.at[d], g_recv.at[d], peer)
        small.start()
        sent.append(small)
    smalls = list(sent)
    offsets_ref[me] = g_ref[...]
    for k in range(steps):
        whole_ref[k, part(me)] = e_ref[k]
    covs_ref[steps - 1] = l_ref[steps - 1]

    def compose(k):
        @pl.loop(0, width // 128)
        def _(tile):
            at = pl.ds(pl.multiple_of(tile * 128, 128), 128)
            after = whole_ref[steps - 1] if k == steps - 2 else gains_ref[k + 1]
            gains_ref[k, at] = three_pass(whole_ref[k, at], after, 0)

    for k in range(steps - 2, -1, -1):
        complete(k)
        pump(2)
        columns_ref[k] = three_pass(whole_ref[k], covs_ref[k + 1], 1)
        swaps = []
        for d, peer in enumerate(peers):
            swap = copy(
                columns_ref.at[k, part(peer)], pieces_ref.at[k, me],
                z_send.at[k, d], z_recv.at[k, d], peer,
            )
            swap.start()
            swaps.append(swap)
        pieces_ref[k, me] = columns_ref[k, part(me)]
        if k == steps - 2:
            complete(steps - 1)
            pump(1)
        if k > 0:
            compose(k)
        for swap in swaps:
            swap.wait_recv()
        sent.extend(swaps)
        pieces = jnp.concatenate([pieces_ref[k, p] for p in range(n)], axis=1)
        covs_ref[k] = three_pass(pieces, whole_ref[k], 1) + l_ref[k]

    cov_ref[part(me)] = covs_ref[0]
    for hop in range(n - 1):
        owner = lax.rem(me - hop + n, n)
        source = covs_ref.at[0] if hop == 0 else cov_ref.at[part(owner)]
        move = copy(source, cov_ref.at[part(owner)], c_send.at[hop], c_recv.at[hop], right)
        move.start()
        if hop == 0:
            compose(0)
        move.wait_recv()
        sent.append(move)
    for small in smalls:
        small.wait_recv()
    for move in [*ring.values(), *sent]:
        move.wait_send()


def block_element(transitions, offsets, noise_cov):
    steps, rows, width = transitions.shape
    n = lax.axis_size("panel")
    f32 = jnp.float32
    vmem = pl.BlockSpec(memory_space=pltpu.VMEM)
    dma = pltpu.SemaphoreType.DMA
    return pl.pallas_call(
        functools.partial(block_kernel, n),
        out_shape=(
            jax.ShapeDtypeStruct((steps, width, width), f32),
            jax.ShapeDtypeStruct((steps - 1, width, width), f32),
            jax.ShapeDtypeStruct((steps, rows, width), f32),
            jax.ShapeDtypeStruct((width, width), f32),
            jax.ShapeDtypeStruct((n, steps, rows), f32),
        ),
        in_specs=[vmem] * 3,
        out_specs=(vmem,) * 5,
        scratch_shapes=[
            pltpu.VMEM((steps - 1, width, rows), f32),
            pltpu.VMEM((steps - 1, n, rows, rows), f32),
            dma((steps, n - 1)), dma((steps, n - 1)),
            dma((steps - 1, n - 1)), dma((steps - 1, n - 1)),
            dma((n - 1,)), dma((n - 1,)), dma((n - 1,)), dma((n - 1,)),
        ],
        compiler_params=pltpu.CompilerParams(
            collective_id=0, has_side_effects=True, vmem_limit_bytes=48 * 2**20
        ),
        cost_estimate=pl.CostEstimate(
            flops=18 * width**3, bytes_accessed=12 * 2**20, transcendentals=0
        ),
    )(transitions, offsets, noise_cov)


def send(value, pairs):
    return lax.ppermute(value, "tm", pairs)


def spread(value, core, distance, blocks, groups):
    half = value.shape[0] // 2
    own = jnp.where(core == 0, value[:half], value[half:])
    got = None
    for pair in range(distance // 2):
        pairs = [
            (base + distance + c, base + 2 * pair + c) for base in groups for c in range(2)
        ]
        part = send(own, pairs)
        got = part if got is None else got + part
    other = send(got, [(t, t ^ 1) for t in range(blocks)])
    return jnp.where(
        core == 0, jnp.concatenate([got, other]), jnp.concatenate([other, got])
    )


def later_state(gains, offsets, covs):
    blocks = lax.axis_size("tm")
    me = lax.axis_index("tm")
    core = me % 2
    swap = [(t, t ^ 1) for t in range(blocks)]
    r_gain, r_offset, r_cov = send(gains, swap), send(offsets, swap), send(covs, swap)
    lower = core == 0
    eye = jnp.eye(gains.shape[0], dtype=jnp.float32)
    x_gain = jnp.where(lower, r_gain, eye)
    x_offset = jnp.where(lower, r_offset, 0.0)
    x_cov = jnp.where(lower, r_cov, 0.0)
    first = jnp.where(lower, gains, r_gain)
    g_offset = matvec(first, jnp.where(lower, r_offset, offsets)) + jnp.where(
        lower, offsets, r_offset
    )
    g_cov = product_t(product(first, jnp.where(lower, r_cov, covs)), first) + jnp.where(
        lower, covs, r_cov
    )
    g_gain = product(first, jnp.where(lower, r_gain, gains))
    distance = 2
    while distance < blocks:
        last = 2 * distance == blocks
        groups = list(range(0, blocks, 2 * distance))
        r_cov = spread(g_cov, core, distance, blocks, groups)
        r_offset = spread(g_offset, core, distance, blocks, groups)
        lower = (me // distance) % 2 == 0
        new_cov = product_t(product(x_gain, r_cov), x_gain) + x_cov
        new_offset = matvec(x_gain, r_offset) + x_offset
        if not last:
            r_gain = spread(g_gain, core, distance, blocks, groups[:-1])
            g_offset = matvec(g_gain, r_offset) + g_offset
            g_cov = product_t(product(g_gain, r_cov), g_gain) + g_cov
            g_gain = product(g_gain, r_gain)
            x_gain = jnp.where(lower, product(x_gain, r_gain), x_gain)
        x_cov = jnp.where(lower, new_cov, x_cov)
        x_offset = jnp.where(lower, new_offset, x_offset)
        distance *= 2
    return x_offset, x_cov


def per_device(transitions, offsets, noise_cov):
    steps, rows = transitions.shape[:2]
    start = lax.axis_index("panel") * rows
    if rows % 128 == 0 and steps > 1:
        whole, composed, covs, whole_cov, parts = block_element(
            transitions, offsets, noise_cov
        )
        all_offsets = jnp.swapaxes(parts, 0, 1).reshape(steps, -1)
        gains = [whole[steps - 1], *(composed[k] for k in range(steps - 2, -1, -1))]
        means = [all_offsets[steps - 1]]
        for k in range(steps - 2, -1, -1):
            means.append(matvec(whole[k], means[-1]) + all_offsets[k])
        covs = [covs[k] for k in range(steps - 1, -1, -1)]
        gain, offset = gains[-1], means[-1]
    else:
        whole = {}
        for k in [*range(steps - 2, -1, -1), steps - 1]:
            whole[k] = lax.all_gather(transitions[k], "panel", axis=0, tiled=True)
        all_offsets = lax.all_gather(offsets, "panel", axis=1, tiled=True)
        cov = noise_cov[steps - 1]
        offset = all_offsets[steps - 1]
        gain = whole[steps - 1]
        covs, gains, means = [cov], [gain], [offset]
        for k in range(steps - 2, -1, -1):
            columns = product_t(whole[k], cov)
            mine = lax.all_to_all(columns, "panel", split_axis=0, concat_axis=1, tiled=True)
            cov = product_t(mine, whole[k]) + noise_cov[k]
            gain = product(whole[k], gain)
            offset = matvec(whole[k], offset) + all_offsets[k]
            covs.append(cov)
            gains.append(gain)
            means.append(offset)
        whole_cov = lax.all_gather(cov, "panel", axis=0, tiled=True)
    next_mean, next_cov = later_state(gain, offset, whole_cov)
    covs, gains, means = covs[::-1], gains[::-1], means[::-1]
    own = jnp.concatenate([lax.dynamic_slice_in_dim(f, start, rows, 0) for f in gains])
    own_offsets = jnp.concatenate(
        [lax.dynamic_slice_in_dim(m, start, rows, 0) for m in means]
    )
    mean = (matvec(own, next_mean) + own_offsets).reshape(steps, rows)
    left = product(own, next_cov).reshape(steps, rows, -1)
    out = jnp.stack([product_t(left[k], gains[k]) + covs[k] for k in range(steps)])
    return mean, out


def solution(mesh):
    placed = (P("tm", "panel", None), P("tm", "panel"), P("tm", "panel", None))
    return jax.shard_map(
        per_device,
        mesh=mesh,
        in_specs=placed,
        out_specs=(P("tm", "panel"), P("tm", "panel", None)),
        check_vma=False,
    )
```

```python
import functools

import jax
import jax.numpy as jnp
from jax import lax
from jax.experimental import pallas as pl
from jax.experimental.pallas import tpu as pltpu
from jax.sharding import PartitionSpec as P


def product(left, right):
    return jnp.dot(left, right, precision=lax.Precision.HIGH, preferred_element_type=jnp.float32)


def product_t(left, right):
    return lax.dot_general(
        left, right, (((1,), (1,)), ((), ())),
        precision=lax.Precision.HIGH, preferred_element_type=jnp.float32,
    )


def matvec(matrix, vector):
    return jnp.sum(matrix * vector[None, :], axis=1)


def halves(value):
    high = value.astype(jnp.bfloat16)
    return high, (value - high.astype(jnp.float32)).astype(jnp.bfloat16)


def three_pass(left, right, across):
    dims = (((1,), (across,)), ((), ()))
    left_high, left_low = halves(left)
    right_high, right_low = halves(right)

    def dot(a, b):
        return lax.dot_general(a, b, dims, preferred_element_type=jnp.float32)

    return dot(left_high, right_high) + (dot(left_high, right_low) + dot(left_low, right_high))


def send_order(steps, hops):
    order, reached, at = [], [0] * steps, [-2] * steps
    while len(order) < steps * hops:
        ready = [k for k in range(steps) if reached[k] < hops]
        k = next((k for k in ready if at[k] <= len(order) - 2), ready[0])
        order.append((k, reached[k]))
        reached[k] += 1
        at[k] = len(order) - 1
    return order


def block_kernel(
    n, e_ref, g_ref, l_ref, whole_ref, own_ref, covs_ref, cov_ref, offsets_ref, *more
):
    steps, rows, width = e_ref.shape
    gains = more[: steps - 1]
    (columns_ref, pieces_ref, e_send, e_recv, z_send, z_recv, c_send, c_recv, g_send,
     g_recv) = more[steps - 1 :]
    me = lax.axis_index("panel")
    right = lax.rem(me + 1, n)
    peers = [lax.rem(me + d, n) for d in range(1, n)]

    def part(owner):
        return pl.ds(pl.multiple_of(owner * rows, rows), rows)

    def copy(source, target, send_sem, recv_sem, peer):
        return pltpu.make_async_remote_copy(
            src_ref=source, dst_ref=target, send_sem=send_sem, recv_sem=recv_sem,
            device_id={"panel": peer}, device_id_type=pl.DeviceIdType.MESH,
        )

    barrier = pltpu.get_barrier_semaphore()
    for peer in peers:
        pl.semaphore_signal(
            barrier, inc=1, device_id={"panel": peer}, device_id_type=pl.DeviceIdType.MESH
        )
    pl.semaphore_wait(barrier, n - 1)

    arrival = [steps - 2, steps - 1, *range(steps - 3, -1, -1)]
    order = [(arrival[k], hop) for k, hop in send_order(steps, n - 1)]
    ring, landed, sent = {}, set(), []

    def land(k, hop):
        if (k, hop) not in landed:
            ring[k, hop].wait_recv()
            landed.add((k, hop))

    def pump(count):
        for _ in range(min(count, len(order) - len(ring))):
            k, hop = order[len(ring)]
            owner = lax.rem(me - hop + n, n)
            if hop > 0:
                land(k, hop - 1)
            source = e_ref.at[k] if hop == 0 else whole_ref.at[k, part(owner)]
            ring[k, hop] = copy(
                source, whole_ref.at[k, part(owner)], e_send.at[k, hop], e_recv.at[k, hop], right
            )
            ring[k, hop].start()

    def complete(k):
        while (k, n - 2) not in ring:
            pump(1)
        land(k, n - 2)

    pump(2)
    for d, peer in enumerate(peers):
        small = copy(g_ref, offsets_ref.at[me], g_send.at[d], g_recv.at[d], peer)
        small.start()
        sent.append(small)
    smalls = list(sent)
    offsets_ref[me] = g_ref[...]
    for k in range(steps):
        whole_ref[k, part(me)] = e_ref[k]
    covs_ref[steps - 1] = l_ref[steps - 1]

    def compose(k):
        @pl.loop(0, width // 128)
        def _(tile):
            at = pl.ds(pl.multiple_of(tile * 128, 128), 128)
            after = whole_ref[steps - 1] if k == steps - 2 else gains[k + 1][...]
            gains[k][at] = three_pass(whole_ref[k, at], after, 0)

    for k in range(steps - 2, -1, -1):
        complete(k)
        pump(2)
        columns_ref[k] = three_pass(whole_ref[k], covs_ref[k + 1], 1)
        swaps = []
        for d, peer in enumerate(peers):
            swap = copy(
                columns_ref.at[k, part(peer)], pieces_ref.at[k, me],
                z_send.at[k, d], z_recv.at[k, d], peer,
            )
            swap.start()
            swaps.append(swap)
        pieces_ref[k, me] = columns_ref[k, part(me)]
        if k == steps - 2:
            complete(steps - 1)
            pump(1)
        if k > 0:
            compose(k)
        for swap in swaps:
            swap.wait_recv()
        sent.extend(swaps)
        pieces = jnp.concatenate([pieces_ref[k, p] for p in range(n)], axis=1)
        covs_ref[k] = three_pass(pieces, whole_ref[k], 1) + l_ref[k]

    kept = n // 2 + 1
    for j in range(kept):
        at = part(lax.rem(me + j, n))
        cov_ref[part(me), at] = covs_ref[0, :, at]
    for hop in range(n - 1):
        owner = lax.rem(me - hop + n, n)
        moves = []
        for j in range(kept):
            at = part(lax.rem(owner + j, n))
            source = covs_ref.at[0, :, at] if hop == 0 else cov_ref.at[part(owner), at]
            move = copy(
                source, cov_ref.at[part(owner), at], c_send.at[hop, j], c_recv.at[hop, j], right
            )
            move.start()
            moves.append(move)
        if hop == 0:
            compose(0)
        for move in moves:
            move.wait_recv()
        sent.extend(moves)
    for p in range(n):
        for j in range(kept, n):
            q = (p + j) % n
            cov_ref[p * rows : (p + 1) * rows, q * rows : (q + 1) * rows] = cov_ref[
                q * rows : (q + 1) * rows, p * rows : (p + 1) * rows
            ].T
    own_ref[steps - 1] = e_ref[steps - 1]
    for k in range(steps - 1):
        own_ref[k] = gains[k][part(me)]
    for small in smalls:
        small.wait_recv()
    for move in [*ring.values(), *sent]:
        move.wait_send()


def block_element(transitions, offsets, noise_cov):
    steps, rows, width = transitions.shape
    n = lax.axis_size("panel")
    f32 = jnp.float32
    vmem = pl.BlockSpec(memory_space=pltpu.VMEM)
    dma = pltpu.SemaphoreType.DMA
    return pl.pallas_call(
        functools.partial(block_kernel, n),
        out_shape=(
            jax.ShapeDtypeStruct((steps, width, width), f32),
            jax.ShapeDtypeStruct((steps, rows, width), f32),
            jax.ShapeDtypeStruct((steps, rows, width), f32),
            jax.ShapeDtypeStruct((width, width), f32),
            jax.ShapeDtypeStruct((n, steps, rows), f32),
            *[jax.ShapeDtypeStruct((width, width), f32)] * (steps - 1),
        ),
        in_specs=[vmem] * 3,
        out_specs=(vmem,) * (steps + 4),
        scratch_shapes=[
            pltpu.VMEM((steps - 1, width, rows), f32),
            pltpu.VMEM((steps - 1, n, rows, rows), f32),
            dma((steps, n - 1)), dma((steps, n - 1)),
            dma((steps - 1, n - 1)), dma((steps - 1, n - 1)),
            dma((n - 1, n // 2 + 1)), dma((n - 1, n // 2 + 1)), dma((n - 1,)), dma((n - 1,)),
        ],
        compiler_params=pltpu.CompilerParams(
            collective_id=0, has_side_effects=True, vmem_limit_bytes=48 * 2**20
        ),
        cost_estimate=pl.CostEstimate(
            flops=18 * width**3, bytes_accessed=12 * 2**20, transcendentals=0
        ),
    )(transitions, offsets, noise_cov)


def send(value, pairs):
    return lax.ppermute(value, "tm", pairs)


def spread(value, core, distance, blocks, groups):
    half = value.shape[0] // 2
    own = jnp.where(core == 0, value[:half], value[half:])
    got = None
    for pair in range(distance // 2):
        pairs = [
            (base + distance + c, base + 2 * pair + c) for base in groups for c in range(2)
        ]
        part = send(own, pairs)
        got = part if got is None else got + part
    other = send(got, [(t, t ^ 1) for t in range(blocks)])
    return jnp.where(
        core == 0, jnp.concatenate([got, other]), jnp.concatenate([other, got])
    )


def later_state(gains, offsets, covs):
    blocks = lax.axis_size("tm")
    me = lax.axis_index("tm")
    core = me % 2
    swap = [(t, t ^ 1) for t in range(blocks)]
    r_gain, r_offset, r_cov = send(gains, swap), send(offsets, swap), send(covs, swap)
    lower = core == 0
    eye = jnp.eye(gains.shape[0], dtype=jnp.float32)
    x_gain = jnp.where(lower, r_gain, eye)
    x_offset = jnp.where(lower, r_offset, 0.0)
    x_cov = jnp.where(lower, r_cov, 0.0)
    first = jnp.where(lower, gains, r_gain)
    g_offset = matvec(first, jnp.where(lower, r_offset, offsets)) + jnp.where(
        lower, offsets, r_offset
    )
    g_cov = product_t(product(first, jnp.where(lower, r_cov, covs)), first) + jnp.where(
        lower, covs, r_cov
    )
    g_gain = product(first, jnp.where(lower, r_gain, gains))
    distance = 2
    while distance < blocks:
        last = 2 * distance == blocks
        groups = list(range(0, blocks, 2 * distance))
        r_cov = spread(g_cov, core, distance, blocks, groups)
        r_offset = spread(g_offset, core, distance, blocks, groups)
        lower = (me // distance) % 2 == 0
        new_cov = product_t(product(x_gain, r_cov), x_gain) + x_cov
        new_offset = matvec(x_gain, r_offset) + x_offset
        if not last:
            r_gain = spread(g_gain, core, distance, blocks, groups[:-1])
            g_offset = matvec(g_gain, r_offset) + g_offset
            g_cov = product_t(product(g_gain, r_cov), g_gain) + g_cov
            g_gain = product(g_gain, r_gain)
            x_gain = jnp.where(lower, product(x_gain, r_gain), x_gain)
        x_cov = jnp.where(lower, new_cov, x_cov)
        x_offset = jnp.where(lower, new_offset, x_offset)
        distance *= 2
    return x_offset, x_cov


def per_device(transitions, offsets, noise_cov):
    steps, rows = transitions.shape[:2]
    start = lax.axis_index("panel") * rows
    if rows % 128 == 0 and steps > 1:
        whole, own, covs, whole_cov, parts, *composed = block_element(
            transitions, offsets, noise_cov
        )
        all_offsets = jnp.swapaxes(parts, 0, 1).reshape(steps, -1)
        gains = [whole[steps - 1], *(composed[k] for k in range(steps - 2, -1, -1))]
        means = [all_offsets[steps - 1]]
        for k in range(steps - 2, -1, -1):
            means.append(matvec(whole[k], means[-1]) + all_offsets[k])
        covs = [covs[k] for k in range(steps - 1, -1, -1)]
        gain, offset = gains[-1], means[-1]
        own = own.reshape(steps * rows, -1)
    else:
        whole = {}
        for k in [*range(steps - 2, -1, -1), steps - 1]:
            whole[k] = lax.all_gather(transitions[k], "panel", axis=0, tiled=True)
        all_offsets = lax.all_gather(offsets, "panel", axis=1, tiled=True)
        cov = noise_cov[steps - 1]
        offset = all_offsets[steps - 1]
        gain = whole[steps - 1]
        covs, gains, means = [cov], [gain], [offset]
        for k in range(steps - 2, -1, -1):
            columns = product_t(whole[k], cov)
            mine = lax.all_to_all(columns, "panel", split_axis=0, concat_axis=1, tiled=True)
            cov = product_t(mine, whole[k]) + noise_cov[k]
            gain = product(whole[k], gain)
            offset = matvec(whole[k], offset) + all_offsets[k]
            covs.append(cov)
            gains.append(gain)
            means.append(offset)
        whole_cov = lax.all_gather(cov, "panel", axis=0, tiled=True)
        own = jnp.concatenate(
            [lax.dynamic_slice_in_dim(f, start, rows, 0) for f in gains[::-1]]
        )
    next_mean, next_cov = later_state(gain, offset, whole_cov)
    covs, gains, means = covs[::-1], gains[::-1], means[::-1]
    own_offsets = jnp.concatenate(
        [lax.dynamic_slice_in_dim(m, start, rows, 0) for m in means]
    )
    mean = (matvec(own, next_mean) + own_offsets).reshape(steps, rows)
    left = product(own, next_cov).reshape(steps, rows, -1)
    out = jnp.stack([product_t(left[k], gains[k]) + covs[k] for k in range(steps)])
    return mean, out


def solution(mesh):
    placed = (P("tm", "panel", None), P("tm", "panel"), P("tm", "panel", None))
    return jax.shard_map(
        per_device,
        mesh=mesh,
        in_specs=placed,
        out_specs=(P("tm", "panel"), P("tm", "panel", None)),
        check_vma=False,
    )
```

```python
import functools

import jax
import jax.numpy as jnp
from jax import lax
from jax.experimental import pallas as pl
from jax.experimental.pallas import tpu as pltpu
from jax.sharding import PartitionSpec as P


def product(left, right):
    return jnp.dot(left, right, precision=lax.Precision.HIGH, preferred_element_type=jnp.float32)


def product_t(left, right):
    return lax.dot_general(
        left, right, (((1,), (1,)), ((), ())),
        precision=lax.Precision.HIGH, preferred_element_type=jnp.float32,
    )


def matvec(matrix, vector):
    return jnp.sum(matrix * vector[None, :], axis=1)


def halves(value):
    high = value.astype(jnp.bfloat16)
    return high, (value - high.astype(jnp.float32)).astype(jnp.bfloat16)


def three_pass(left, right, across):
    dims = (((1,), (across,)), ((), ()))
    left_high, left_low = halves(left)
    right_high, right_low = halves(right)

    def dot(a, b):
        return lax.dot_general(a, b, dims, preferred_element_type=jnp.float32)

    return dot(left_high, right_high) + (dot(left_high, right_low) + dot(left_low, right_high))


def send_order(steps, hops):
    sends = [(k, hop) for hop in range(hops) for k in range(steps)]
    return sorted(sends, key=lambda send: 3 * send[1] + send[0] + send[0] // 3)


def block_kernel(
    n, e_ref, g_ref, l_ref, whole_ref, own_ref, covs_ref, cov_ref, offsets_ref, *more
):
    steps, rows, width = e_ref.shape
    gains = more[: steps - 1]
    (columns_ref, pieces_ref, e_send, e_recv, z_send, z_recv, c_send, c_recv, g_send,
     g_recv) = more[steps - 1 :]
    me = lax.axis_index("panel")
    right = lax.rem(me + 1, n)
    peers = [lax.rem(me + d, n) for d in range(1, n)]

    def part(owner):
        return pl.ds(pl.multiple_of(owner * rows, rows), rows)

    def copy(source, target, send_sem, recv_sem, peer):
        return pltpu.make_async_remote_copy(
            src_ref=source, dst_ref=target, send_sem=send_sem, recv_sem=recv_sem,
            device_id={"panel": peer}, device_id_type=pl.DeviceIdType.MESH,
        )

    barrier = pltpu.get_barrier_semaphore()
    for peer in peers:
        pl.semaphore_signal(
            barrier, inc=1, device_id={"panel": peer}, device_id_type=pl.DeviceIdType.MESH
        )
    pl.semaphore_wait(barrier, n - 1)

    arrival = [steps - 2, steps - 1, *range(steps - 3, -1, -1)]
    order = [(arrival[k], hop) for k, hop in send_order(steps, n - 1)]
    ring, landed, sent = {}, set(), []

    def land(k, hop):
        if (k, hop) not in landed:
            ring[k, hop].wait_recv()
            landed.add((k, hop))

    def pump(count):
        for _ in range(min(count, len(order) - len(ring))):
            k, hop = order[len(ring)]
            owner = lax.rem(me - hop + n, n)
            if hop > 0:
                land(k, hop - 1)
            source = e_ref.at[k] if hop == 0 else whole_ref.at[k, part(owner)]
            ring[k, hop] = copy(
                source, whole_ref.at[k, part(owner)], e_send.at[k, hop], e_recv.at[k, hop], right
            )
            ring[k, hop].start()

    def complete(k):
        while (k, n - 2) not in ring:
            pump(1)
        land(k, n - 2)

    pump(3)
    for d, peer in enumerate(peers):
        small = copy(g_ref, offsets_ref.at[me], g_send.at[d], g_recv.at[d], peer)
        small.start()
        sent.append(small)
    smalls = list(sent)
    offsets_ref[me] = g_ref[...]
    for k in range(steps):
        whole_ref[k, part(me)] = e_ref[k]
    covs_ref[steps - 1] = l_ref[steps - 1]

    def compose(k):
        @pl.loop(0, width // 128)
        def _(tile):
            at = pl.ds(pl.multiple_of(tile * 128, 128), 128)
            after = whole_ref[steps - 1] if k == steps - 2 else gains[k + 1][...]
            gains[k][at] = three_pass(whole_ref[k, at], after, 0)

    for k in range(steps - 2, -1, -1):
        complete(k)
        pump(3)
        columns_ref[k] = three_pass(whole_ref[k], covs_ref[k + 1], 1)
        swaps = []
        for d, peer in enumerate(peers):
            swap = copy(
                columns_ref.at[k, part(peer)], pieces_ref.at[k, me],
                z_send.at[k, d], z_recv.at[k, d], peer,
            )
            swap.start()
            swaps.append(swap)
        pieces_ref[k, me] = columns_ref[k, part(me)]
        if k == steps - 2:
            complete(steps - 1)
            pump(len(order))
            compose(k)
        for swap in swaps:
            swap.wait_recv()
        sent.extend(swaps)
        pieces = jnp.concatenate([pieces_ref[k, p] for p in range(n)], axis=1)
        covs_ref[k] = three_pass(pieces, whole_ref[k], 1) + l_ref[k]

    kept = n // 2 + 1
    later = list(range(steps - 3, -1, -1))
    for j in range(kept):
        at = part(lax.rem(me + j, n))
        cov_ref[part(me), at] = covs_ref[0, :, at]
    for hop in range(n - 1):
        owner = lax.rem(me - hop + n, n)
        moves = []
        for j in range(kept):
            at = part(lax.rem(owner + j, n))
            source = covs_ref.at[0, :, at] if hop == 0 else cov_ref.at[part(owner), at]
            move = copy(
                source, cov_ref.at[part(owner), at], c_send.at[hop, j], c_recv.at[hop, j], right
            )
            move.start()
            moves.append(move)
        if later:
            compose(later.pop(0))
        for move in moves:
            move.wait_recv()
        sent.extend(moves)
    for k in later:
        compose(k)
    for p in range(n):
        for j in range(kept, n):
            q = (p + j) % n
            cov_ref[p * rows : (p + 1) * rows, q * rows : (q + 1) * rows] = cov_ref[
                q * rows : (q + 1) * rows, p * rows : (p + 1) * rows
            ].T
    own_ref[steps - 1] = e_ref[steps - 1]
    for k in range(steps - 1):
        own_ref[k] = gains[k][part(me)]
    for small in smalls:
        small.wait_recv()
    for move in [*ring.values(), *sent]:
        move.wait_send()


def block_element(transitions, offsets, noise_cov):
    steps, rows, width = transitions.shape
    n = lax.axis_size("panel")
    f32 = jnp.float32
    vmem = pl.BlockSpec(memory_space=pltpu.VMEM)
    dma = pltpu.SemaphoreType.DMA
    return pl.pallas_call(
        functools.partial(block_kernel, n),
        out_shape=(
            jax.ShapeDtypeStruct((steps, width, width), f32),
            jax.ShapeDtypeStruct((steps, rows, width), f32),
            jax.ShapeDtypeStruct((steps, rows, width), f32),
            jax.ShapeDtypeStruct((width, width), f32),
            jax.ShapeDtypeStruct((n, steps, rows), f32),
            *[jax.ShapeDtypeStruct((width, width), f32)] * (steps - 1),
        ),
        in_specs=[vmem] * 3,
        out_specs=(vmem,) * (steps + 4),
        scratch_shapes=[
            pltpu.VMEM((steps - 1, width, rows), f32),
            pltpu.VMEM((steps - 1, n, rows, rows), f32),
            dma((steps, n - 1)), dma((steps, n - 1)),
            dma((steps - 1, n - 1)), dma((steps - 1, n - 1)),
            dma((n - 1, n // 2 + 1)), dma((n - 1, n // 2 + 1)), dma((n - 1,)), dma((n - 1,)),
        ],
        compiler_params=pltpu.CompilerParams(
            collective_id=0, has_side_effects=True, vmem_limit_bytes=48 * 2**20
        ),
        cost_estimate=pl.CostEstimate(
            flops=18 * width**3, bytes_accessed=12 * 2**20, transcendentals=0
        ),
    )(transitions, offsets, noise_cov)


def send(value, pairs):
    return lax.ppermute(value, "tm", pairs)


def spread(value, core, distance, blocks, groups):
    half = value.shape[0] // 2
    own = jnp.where(core == 0, value[:half], value[half:])
    got = None
    for pair in range(distance // 2):
        pairs = [
            (base + distance + c, base + 2 * pair + c) for base in groups for c in range(2)
        ]
        part = send(own, pairs)
        got = part if got is None else got + part
    other = send(got, [(t, t ^ 1) for t in range(blocks)])
    return jnp.where(
        core == 0, jnp.concatenate([got, other]), jnp.concatenate([other, got])
    )


def later_state(gains, offsets, covs):
    blocks = lax.axis_size("tm")
    me = lax.axis_index("tm")
    core = me % 2
    swap = [(t, t ^ 1) for t in range(blocks)]
    r_gain, r_offset, r_cov = send(gains, swap), send(offsets, swap), send(covs, swap)
    lower = core == 0
    eye = jnp.eye(gains.shape[0], dtype=jnp.float32)
    x_gain = jnp.where(lower, r_gain, eye)
    x_offset = jnp.where(lower, r_offset, 0.0)
    x_cov = jnp.where(lower, r_cov, 0.0)
    first = jnp.where(lower, gains, r_gain)
    g_offset = matvec(first, jnp.where(lower, r_offset, offsets)) + jnp.where(
        lower, offsets, r_offset
    )
    g_cov = product_t(product(first, jnp.where(lower, r_cov, covs)), first) + jnp.where(
        lower, covs, r_cov
    )
    g_gain = product(first, jnp.where(lower, r_gain, gains))
    distance = 2
    while distance < blocks:
        last = 2 * distance == blocks
        groups = list(range(0, blocks, 2 * distance))
        r_cov = spread(g_cov, core, distance, blocks, groups)
        r_offset = spread(g_offset, core, distance, blocks, groups)
        lower = (me // distance) % 2 == 0
        new_cov = product_t(product(x_gain, r_cov), x_gain) + x_cov
        new_offset = matvec(x_gain, r_offset) + x_offset
        if not last:
            r_gain = spread(g_gain, core, distance, blocks, groups[:-1])
            g_offset = matvec(g_gain, r_offset) + g_offset
            g_cov = product_t(product(g_gain, r_cov), g_gain) + g_cov
            g_gain = product(g_gain, r_gain)
            x_gain = jnp.where(lower, product(x_gain, r_gain), x_gain)
        x_cov = jnp.where(lower, new_cov, x_cov)
        x_offset = jnp.where(lower, new_offset, x_offset)
        distance *= 2
    return x_offset, x_cov


def per_device(transitions, offsets, noise_cov):
    steps, rows = transitions.shape[:2]
    start = lax.axis_index("panel") * rows
    if rows % 128 == 0 and steps > 1:
        whole, own, covs, whole_cov, parts, *composed = block_element(
            transitions, offsets, noise_cov
        )
        all_offsets = jnp.swapaxes(parts, 0, 1).reshape(steps, -1)
        gains = [whole[steps - 1], *(composed[k] for k in range(steps - 2, -1, -1))]
        means = [all_offsets[steps - 1]]
        for k in range(steps - 2, -1, -1):
            means.append(matvec(whole[k], means[-1]) + all_offsets[k])
        covs = [covs[k] for k in range(steps - 1, -1, -1)]
        gain, offset = gains[-1], means[-1]
        own = own.reshape(steps * rows, -1)
    else:
        whole = {}
        for k in [*range(steps - 2, -1, -1), steps - 1]:
            whole[k] = lax.all_gather(transitions[k], "panel", axis=0, tiled=True)
        all_offsets = lax.all_gather(offsets, "panel", axis=1, tiled=True)
        cov = noise_cov[steps - 1]
        offset = all_offsets[steps - 1]
        gain = whole[steps - 1]
        covs, gains, means = [cov], [gain], [offset]
        for k in range(steps - 2, -1, -1):
            columns = product_t(whole[k], cov)
            mine = lax.all_to_all(columns, "panel", split_axis=0, concat_axis=1, tiled=True)
            cov = product_t(mine, whole[k]) + noise_cov[k]
            gain = product(whole[k], gain)
            offset = matvec(whole[k], offset) + all_offsets[k]
            covs.append(cov)
            gains.append(gain)
            means.append(offset)
        whole_cov = lax.all_gather(cov, "panel", axis=0, tiled=True)
        own = jnp.concatenate(
            [lax.dynamic_slice_in_dim(f, start, rows, 0) for f in gains[::-1]]
        )
    next_mean, next_cov = later_state(gain, offset, whole_cov)
    covs, gains, means = covs[::-1], gains[::-1], means[::-1]
    own_offsets = jnp.concatenate(
        [lax.dynamic_slice_in_dim(m, start, rows, 0) for m in means]
    )
    mean = (matvec(own, next_mean) + own_offsets).reshape(steps, rows)
    left = product(own, next_cov).reshape(steps, rows, -1)
    out = jnp.stack([product_t(left[k], gains[k]) + covs[k] for k in range(steps)])
    return mean, out


def solution(mesh):
    placed = (P("tm", "panel", None), P("tm", "panel"), P("tm", "panel", None))
    return jax.shard_map(
        per_device,
        mesh=mesh,
        in_specs=placed,
        out_specs=(P("tm", "panel"), P("tm", "panel", None)),
        check_vma=False,
    )
```

```python
import functools

import jax
import jax.numpy as jnp
from jax import lax
from jax.experimental import pallas as pl
from jax.experimental.pallas import tpu as pltpu
from jax.sharding import PartitionSpec as P


def product(left, right):
    return jnp.dot(left, right, precision=lax.Precision.HIGH, preferred_element_type=jnp.float32)


def product_t(left, right):
    return lax.dot_general(
        left, right, (((1,), (1,)), ((), ())),
        precision=lax.Precision.HIGH, preferred_element_type=jnp.float32,
    )


def matvec(matrix, vector):
    return jnp.sum(matrix * vector[None, :], axis=1)


def halves(value):
    high = value.astype(jnp.bfloat16)
    return high, (value - high.astype(jnp.float32)).astype(jnp.bfloat16)


def three_pass(left, right, across):
    dims = (((1,), (across,)), ((), ()))
    left_high, left_low = halves(left)
    right_high, right_low = halves(right)

    def dot(a, b):
        return lax.dot_general(a, b, dims, preferred_element_type=jnp.float32)

    return dot(left_high, right_high) + (dot(left_high, right_low) + dot(left_low, right_high))


def send_order(steps, hops):
    sends = [(k, hop) for hop in range(hops) for k in range(steps)]
    return sorted(sends, key=lambda send: 3 * send[1] + send[0] + send[0] // 3)


def block_kernel(
    n, e_ref, g_ref, l_ref, whole_ref, own_ref, covs_ref, cov_ref, offsets_ref, means_ref, *more
):
    steps, rows, width = e_ref.shape
    gains = more[: steps - 1]
    (columns_ref, pieces_ref, e_send, e_recv, z_send, z_recv, c_send, c_recv, g_send,
     g_recv) = more[steps - 1 :]
    me = lax.axis_index("panel")
    right = lax.rem(me + 1, n)
    peers = [lax.rem(me + d, n) for d in range(1, n)]

    def part(owner):
        return pl.ds(pl.multiple_of(owner * rows, rows), rows)

    def copy(source, target, send_sem, recv_sem, peer):
        return pltpu.make_async_remote_copy(
            src_ref=source, dst_ref=target, send_sem=send_sem, recv_sem=recv_sem,
            device_id={"panel": peer}, device_id_type=pl.DeviceIdType.MESH,
        )

    barrier = pltpu.get_barrier_semaphore()
    for peer in peers:
        pl.semaphore_signal(
            barrier, inc=1, device_id={"panel": peer}, device_id_type=pl.DeviceIdType.MESH
        )
    pl.semaphore_wait(barrier, n - 1)

    arrival = [steps - 2, steps - 1, *range(steps - 3, -1, -1)]
    order = [(arrival[k], hop) for k, hop in send_order(steps, n - 1)]
    ring, landed, sent = {}, set(), []

    def land(k, hop):
        if (k, hop) not in landed:
            ring[k, hop].wait_recv()
            landed.add((k, hop))

    def pump(count):
        for _ in range(min(count, len(order) - len(ring))):
            k, hop = order[len(ring)]
            owner = lax.rem(me - hop + n, n)
            if hop > 0:
                land(k, hop - 1)
            source = e_ref.at[k] if hop == 0 else whole_ref.at[k, part(owner)]
            ring[k, hop] = copy(
                source, whole_ref.at[k, part(owner)], e_send.at[k, hop], e_recv.at[k, hop], right
            )
            ring[k, hop].start()

    def complete(k):
        while (k, n - 2) not in ring:
            pump(1)
        land(k, n - 2)

    pump(3)
    for d, peer in enumerate(peers):
        small = copy(g_ref, offsets_ref.at[me], g_send.at[d], g_recv.at[d], peer)
        small.start()
        sent.append(small)
    smalls = list(sent)
    offsets_ref[me] = g_ref[...]
    for k in range(steps):
        whole_ref[k, part(me)] = e_ref[k]
    covs_ref[steps - 1] = l_ref[steps - 1]

    def compose(k):
        @pl.loop(0, width // 128)
        def _(tile):
            at = pl.ds(pl.multiple_of(tile * 128, 128), 128)
            after = whole_ref[steps - 1] if k == steps - 2 else gains[k + 1][...]
            gains[k][at] = three_pass(whole_ref[k, at], after, 0)

    for k in range(steps - 2, -1, -1):
        complete(k)
        pump(3)
        columns_ref[k] = three_pass(whole_ref[k], covs_ref[k + 1], 1)
        swaps = []
        for d, peer in enumerate(peers):
            swap = copy(
                columns_ref.at[k, part(peer)], pieces_ref.at[k, me],
                z_send.at[k, d], z_recv.at[k, d], peer,
            )
            swap.start()
            swaps.append(swap)
        pieces_ref[k, me] = columns_ref[k, part(me)]
        if k == steps - 2:
            complete(steps - 1)
            pump(len(order))
            compose(k)
        for swap in swaps:
            swap.wait_recv()
        sent.extend(swaps)
        pieces = jnp.concatenate([pieces_ref[k, p] for p in range(n)], axis=1)
        covs_ref[k] = three_pass(pieces, whole_ref[k], 1) + l_ref[k]

    kept = n // 2 + 1
    later = list(range(steps - 3, -1, -1))
    for j in range(kept):
        at = part(lax.rem(me + j, n))
        cov_ref[part(me), at] = covs_ref[0, :, at]
    for hop in range(n - 1):
        owner = lax.rem(me - hop + n, n)
        moves = []
        for j in range(kept):
            at = part(lax.rem(owner + j, n))
            source = covs_ref.at[0, :, at] if hop == 0 else cov_ref.at[part(owner), at]
            move = copy(
                source, cov_ref.at[part(owner), at], c_send.at[hop, j], c_recv.at[hop, j], right
            )
            move.start()
            moves.append(move)
        if later:
            compose(later.pop(0))
        for move in moves:
            move.wait_recv()
        sent.extend(moves)
    for k in later:
        compose(k)
    for small in smalls:
        small.wait_recv()
    for k in range(steps - 1, -1, -1):
        row = jnp.concatenate([offsets_ref[p, k : k + 1] for p in range(n)], axis=1)
        row = jnp.broadcast_to(row, (8, width))
        if k < steps - 1:
            row = three_pass(means_ref[k + 1], whole_ref[k], 1) + row
        means_ref[k] = row
    cov_ref[width : width + 8] = means_ref[0]
    cov_ref[width + 8 :] = jnp.zeros((8, width), jnp.float32)
    for p in range(n):
        for j in range(kept, n):
            q = (p + j) % n
            cov_ref[p * rows : (p + 1) * rows, q * rows : (q + 1) * rows] = cov_ref[
                q * rows : (q + 1) * rows, p * rows : (p + 1) * rows
            ].T
    own_ref[steps - 1] = e_ref[steps - 1]
    for k in range(steps - 1):
        own_ref[k] = gains[k][part(me)]
    for move in [*ring.values(), *sent]:
        move.wait_send()


def block_element(transitions, offsets, noise_cov):
    steps, rows, width = transitions.shape
    n = lax.axis_size("panel")
    f32 = jnp.float32
    vmem = pl.BlockSpec(memory_space=pltpu.VMEM)
    dma = pltpu.SemaphoreType.DMA
    return pl.pallas_call(
        functools.partial(block_kernel, n),
        out_shape=(
            jax.ShapeDtypeStruct((steps, width, width), f32),
            jax.ShapeDtypeStruct((steps, rows, width), f32),
            jax.ShapeDtypeStruct((steps, rows, width), f32),
            jax.ShapeDtypeStruct((width + 16, width), f32),
            jax.ShapeDtypeStruct((n, steps, rows), f32),
            jax.ShapeDtypeStruct((steps, 8, width), f32),
            *[jax.ShapeDtypeStruct((width, width), f32)] * (steps - 1),
        ),
        in_specs=[vmem] * 3,
        out_specs=(vmem,) * (steps + 5),
        scratch_shapes=[
            pltpu.VMEM((steps - 1, width, rows), f32),
            pltpu.VMEM((steps - 1, n, rows, rows), f32),
            dma((steps, n - 1)), dma((steps, n - 1)),
            dma((steps - 1, n - 1)), dma((steps - 1, n - 1)),
            dma((n - 1, n // 2 + 1)), dma((n - 1, n // 2 + 1)), dma((n - 1,)), dma((n - 1,)),
        ],
        compiler_params=pltpu.CompilerParams(
            collective_id=0, has_side_effects=True, vmem_limit_bytes=48 * 2**20
        ),
        cost_estimate=pl.CostEstimate(
            flops=18 * width**3, bytes_accessed=12 * 2**20, transcendentals=0
        ),
    )(transitions, offsets, noise_cov)


def scan_kernel(blocks, cov_ref, own_ref, covs_ref, *more):
    steps, rows, width = covs_ref.shape
    gains = more[:steps]
    (out_ref, mean_ref, swap_a, swap_c, first, later_c, g_a, g_c, x_a, x_c, got_a, got_c,
     s_send, s_recv, c_send, c_recv, cw_send, cw_recv, a_send, a_recv, aw_send,
     aw_recv) = more[steps:]
    a_ref = gains[0]
    f32 = jnp.float32
    me = lax.axis_index("tm")
    core = lax.rem(me, 2)
    partner = me + 1 - 2 * core
    tile_rows = 256

    def copy(source, target, send_sem, recv_sem, peer):
        return pltpu.make_async_remote_copy(
            src_ref=source, dst_ref=target, send_sem=send_sem, recv_sem=recv_sem,
            device_id={"tm": peer}, device_id_type=pl.DeviceIdType.MESH,
        )

    def tiles(body):
        @pl.loop(0, width // tile_rows)
        def _(tile):
            body(pl.ds(pl.multiple_of(tile * tile_rows, tile_rows), tile_rows))

    def join(out, gain, cov, add):
        def body(at):
            left = three_pass(gain[at], cov[:width], 0)
            out[at] = three_pass(left, gain[...], 1) + add(at)

        tiles(body)
        tail = pl.ds(width, 8)
        out[tail] = three_pass(cov[tail], gain[...], 1) + add(tail)

    def times(out, left, right):
        def body(at):
            out[at] = three_pass(left[at], right(), 0)

        tiles(body)

    levels = []
    distance = 2
    while distance < blocks:
        levels.append(distance)
        distance *= 2

    def half(ref):
        size = ref.shape[0] // 2
        return ref.at[pl.ds(pl.multiple_of(core * size, 8), size)]

    def place(level):
        return lax.rem(me, 2 * levels[level])

    def holds(level):
        at = place(level)
        return (at >= levels[level]) & (at < levels[level] + 2)

    def lower(level):
        return place(level) < levels[level]

    def inner(level):
        return me < blocks - 2 * levels[level]

    def sends(level, source, target, send_sem, recv_sem):
        d = levels[level]
        return [
            copy(half(source), half(target.at[level]), send_sem.at[level, q],
                 recv_sem.at[level], me - d + 2 * q)
            for q in range(d // 2)
        ]

    def c_sends(level):
        return sends(level, g_c, got_c, c_send, c_recv)

    def a_sends(level):
        return sends(level, g_a, got_a, a_send, a_recv)

    def relay(level, target, send_sem, recv_sem):
        part = half(target.at[level])
        return copy(part, part, send_sem.at[level], recv_sem.at[level], partner)

    def receive(level, target, recv_sem, w_send, w_recv):
        part = half(target.at[level])
        copy(part, part, w_send.at[level], recv_sem.at[level], partner).wait_recv()
        move = relay(level, target, w_send, w_recv)
        move.start()
        move.wait_recv()

    def start_c(level):
        @pl.when(holds(level))
        def _():
            for move in c_sends(level):
                move.start()

    def start_a(level):
        if level < len(levels) - 1:
            @pl.when(holds(level) & inner(level))
            def _():
                for move in a_sends(level):
                    move.start()

    barrier = pltpu.get_barrier_semaphore()
    for d in range(1, blocks):
        pl.semaphore_signal(
            barrier, inc=1, device_id={"tm": lax.rem(me + d, blocks)},
            device_id_type=pl.DeviceIdType.MESH,
        )
    pl.semaphore_wait(barrier, blocks - 1)

    swaps = [
        copy(cov_ref, swap_c, s_send.at[0], s_recv.at[0], partner),
        copy(a_ref, swap_a, s_send.at[1], s_recv.at[1], partner),
    ]
    for move in swaps:
        move.start()
    for move in swaps:
        move.wait_recv()
    early = core == 0
    first[...] = jnp.where(early, a_ref[...], swap_a[...])
    later_c[...] = jnp.where(early, swap_c[...], cov_ref[...])
    g_c[width:] = jnp.zeros((16, width), f32)
    join(g_c, first, later_c, lambda at: jnp.where(early, cov_ref[at], swap_c[at]))
    start_c(0)
    times(g_a, first, lambda: jnp.where(early, swap_a[...], a_ref[...]))
    start_a(0)
    row = lax.broadcasted_iota(jnp.int32, (width, width), 0)
    column = lax.broadcasted_iota(jnp.int32, (width, width), 1)
    x_a[...] = jnp.where(early, swap_a[...], (row == column).astype(f32))
    x_c[...] = jnp.where(early, swap_c[...], 0.0)

    for level in range(len(levels)):
        final = level == len(levels) - 1

        @pl.when(lower(level))
        def _():
            receive(level, got_c, c_recv, cw_send, cw_recv)

        if not final:
            @pl.when(place(level) < 2)
            def _():
                join(g_c, g_a, got_c.at[level], lambda at: g_c[at])

            start_c(level + 1)

        @pl.when(lower(level))
        def _():
            join(x_c, x_a, got_c.at[level], lambda at: x_c[at])

        if not final:
            @pl.when(lower(level) & inner(level))
            def _():
                receive(level, got_a, a_recv, aw_send, aw_recv)
                times(x_a, x_a, lambda: got_a[level])

            @pl.when((place(level) < 2) & inner(level))
            def _():
                times(g_a, g_a, lambda: got_a[level])

            start_a(level + 1)

    for k in range(steps):
        left = three_pass(own_ref[k * rows : (k + 1) * rows], x_c[:width], 0)
        out_ref[k] = three_pass(left, gains[k][...], 1) + covs_ref[k]
    mean_ref[...] = three_pass(x_c[width : width + 8], own_ref[...], 1)

    for move in swaps:
        move.wait_send()
    for level in range(len(levels)):
        @pl.when(holds(level))
        def _():
            for move in c_sends(level):
                move.wait_send()

        @pl.when(lower(level))
        def _():
            relay(level, got_c, cw_send, cw_recv).wait_send()

        if level < len(levels) - 1:
            @pl.when(holds(level) & inner(level))
            def _():
                for move in a_sends(level):
                    move.wait_send()

            @pl.when(lower(level) & inner(level))
            def _():
                relay(level, got_a, aw_send, aw_recv).wait_send()


def scan_and_smooth(cov, own, covs, gains):
    steps, rows, width = covs.shape
    blocks = lax.axis_size("tm")
    f32 = jnp.float32
    vmem = pl.BlockSpec(memory_space=pltpu.VMEM)
    dma = pltpu.SemaphoreType.DMA
    levels = blocks.bit_length() - 2
    square, tall = pltpu.VMEM((width, width), f32), pltpu.VMEM((width + 16, width), f32)
    out, mean = pl.pallas_call(
        functools.partial(scan_kernel, blocks),
        out_shape=(
            jax.ShapeDtypeStruct((steps, rows, width), f32),
            jax.ShapeDtypeStruct((8, steps * rows), f32),
        ),
        in_specs=[vmem] * (3 + steps),
        out_specs=(vmem, vmem),
        scratch_shapes=[
            square, tall, square, tall, square, tall, square, tall,
            pltpu.VMEM((levels, width, width), f32),
            pltpu.VMEM((levels, width + 16, width), f32),
            dma((2,)), dma((2,)), dma((levels, blocks // 4)), dma((levels,)),
            dma((levels,)), dma((levels,)), dma((levels, blocks // 4)), dma((levels,)),
            dma((levels,)), dma((levels,)),
        ],
        compiler_params=pltpu.CompilerParams(
            collective_id=1, has_side_effects=True, vmem_limit_bytes=48 * 2**20
        ),
        cost_estimate=pl.CostEstimate(
            flops=24 * width**3, bytes_accessed=12 * 2**20, transcendentals=0
        ),
    )(cov, own, covs, *gains)
    return mean, out


def send(value, pairs):
    return lax.ppermute(value, "tm", pairs)


def spread(value, core, distance, blocks, groups):
    half = value.shape[0] // 2
    own = jnp.where(core == 0, value[:half], value[half:])
    got = None
    for pair in range(distance // 2):
        pairs = [
            (base + distance + c, base + 2 * pair + c) for base in groups for c in range(2)
        ]
        part = send(own, pairs)
        got = part if got is None else got + part
    other = send(got, [(t, t ^ 1) for t in range(blocks)])
    return jnp.where(
        core == 0, jnp.concatenate([got, other]), jnp.concatenate([other, got])
    )


def later_state(gains, offsets, covs):
    blocks = lax.axis_size("tm")
    me = lax.axis_index("tm")
    core = me % 2
    swap = [(t, t ^ 1) for t in range(blocks)]
    r_gain, r_offset, r_cov = send(gains, swap), send(offsets, swap), send(covs, swap)
    lower = core == 0
    eye = jnp.eye(gains.shape[0], dtype=jnp.float32)
    x_gain = jnp.where(lower, r_gain, eye)
    x_offset = jnp.where(lower, r_offset, 0.0)
    x_cov = jnp.where(lower, r_cov, 0.0)
    first = jnp.where(lower, gains, r_gain)
    g_offset = matvec(first, jnp.where(lower, r_offset, offsets)) + jnp.where(
        lower, offsets, r_offset
    )
    g_cov = product_t(product(first, jnp.where(lower, r_cov, covs)), first) + jnp.where(
        lower, covs, r_cov
    )
    g_gain = product(first, jnp.where(lower, r_gain, gains))
    distance = 2
    while distance < blocks:
        last = 2 * distance == blocks
        groups = list(range(0, blocks, 2 * distance))
        r_cov = spread(g_cov, core, distance, blocks, groups)
        r_offset = spread(g_offset, core, distance, blocks, groups)
        lower = (me // distance) % 2 == 0
        new_cov = product_t(product(x_gain, r_cov), x_gain) + x_cov
        new_offset = matvec(x_gain, r_offset) + x_offset
        if not last:
            r_gain = spread(g_gain, core, distance, blocks, groups[:-1])
            g_offset = matvec(g_gain, r_offset) + g_offset
            g_cov = product_t(product(g_gain, r_cov), g_gain) + g_cov
            g_gain = product(g_gain, r_gain)
            x_gain = jnp.where(lower, product(x_gain, r_gain), x_gain)
        x_cov = jnp.where(lower, new_cov, x_cov)
        x_offset = jnp.where(lower, new_offset, x_offset)
        distance *= 2
    return x_offset, x_cov


def per_device(transitions, offsets, noise_cov):
    steps, rows = transitions.shape[:2]
    start = lax.axis_index("panel") * rows
    if rows % 128 == 0 and steps > 1 and lax.axis_size("tm") > 2:
        whole, own, covs, whole_cov, _, means, *composed = block_element(
            transitions, offsets, noise_cov
        )
        gains = [*composed, whole[steps - 1]]
        mean, out = scan_and_smooth(whole_cov, own.reshape(steps * rows, -1), covs, gains)
        rows_mean = lax.dynamic_slice_in_dim(means[:, 0], start, rows, 1)
        return mean[0].reshape(steps, rows) + rows_mean, out
    else:
        whole = {}
        for k in [*range(steps - 2, -1, -1), steps - 1]:
            whole[k] = lax.all_gather(transitions[k], "panel", axis=0, tiled=True)
        all_offsets = lax.all_gather(offsets, "panel", axis=1, tiled=True)
        cov = noise_cov[steps - 1]
        offset = all_offsets[steps - 1]
        gain = whole[steps - 1]
        covs, gains, means = [cov], [gain], [offset]
        for k in range(steps - 2, -1, -1):
            columns = product_t(whole[k], cov)
            mine = lax.all_to_all(columns, "panel", split_axis=0, concat_axis=1, tiled=True)
            cov = product_t(mine, whole[k]) + noise_cov[k]
            gain = product(whole[k], gain)
            offset = matvec(whole[k], offset) + all_offsets[k]
            covs.append(cov)
            gains.append(gain)
            means.append(offset)
        whole_cov = lax.all_gather(cov, "panel", axis=0, tiled=True)
        own = jnp.concatenate(
            [lax.dynamic_slice_in_dim(f, start, rows, 0) for f in gains[::-1]]
        )
    next_mean, next_cov = later_state(gain, offset, whole_cov)
    covs, gains, means = covs[::-1], gains[::-1], means[::-1]
    own_offsets = jnp.concatenate(
        [lax.dynamic_slice_in_dim(m, start, rows, 0) for m in means]
    )
    mean = (matvec(own, next_mean) + own_offsets).reshape(steps, rows)
    left = product(own, next_cov).reshape(steps, rows, -1)
    out = jnp.stack([product_t(left[k], gains[k]) + covs[k] for k in range(steps)])
    return mean, out


def solution(mesh):
    placed = (P("tm", "panel", None), P("tm", "panel"), P("tm", "panel", None))
    return jax.shard_map(
        per_device,
        mesh=mesh,
        in_specs=placed,
        out_specs=(P("tm", "panel"), P("tm", "panel", None)),
        check_vma=False,
    )
```

```python
import functools

import jax
import jax.numpy as jnp
from jax import lax
from jax.experimental import pallas as pl
from jax.experimental.pallas import tpu as pltpu
from jax.sharding import PartitionSpec as P


def product(left, right):
    return jnp.dot(left, right, precision=lax.Precision.HIGH, preferred_element_type=jnp.float32)


def product_t(left, right):
    return lax.dot_general(
        left, right, (((1,), (1,)), ((), ())),
        precision=lax.Precision.HIGH, preferred_element_type=jnp.float32,
    )


def matvec(matrix, vector):
    return jnp.sum(matrix * vector[None, :], axis=1)


def halves(value):
    high = value.astype(jnp.bfloat16)
    return high, (value - high.astype(jnp.float32)).astype(jnp.bfloat16)


def three_pass(left, right, across):
    dims = (((1,), (across,)), ((), ()))
    left_high, left_low = halves(left)
    right_high, right_low = halves(right)

    def dot(a, b):
        return lax.dot_general(a, b, dims, preferred_element_type=jnp.float32)

    return dot(left_high, right_high) + (dot(left_high, right_low) + dot(left_low, right_high))


def send_order(steps, hops):
    sends = [(k, hop) for hop in range(hops) for k in range(steps)]
    return sorted(sends, key=lambda send: 3 * send[1] + send[0] + 4 * (send[0] // 3))


def block_kernel(
    n, e_ref, g_ref, l_ref, last_ref, own_ref, covs_ref, cov_ref, offsets_ref, means_ref, *more
):
    steps, rows, width = e_ref.shape
    gains = more[: steps - 1]
    (whole_ref, columns_ref, pieces_ref, e_send, e_recv, z_send, z_recv, c_send, c_recv, g_send,
     g_recv) = more[steps - 1 :]
    me = lax.axis_index("panel")
    right = lax.rem(me + 1, n)
    peers = [lax.rem(me + d, n) for d in range(1, n)]

    def part(owner):
        return pl.ds(pl.multiple_of(owner * rows, rows), rows)

    def copy(source, target, send_sem, recv_sem, peer):
        return pltpu.make_async_remote_copy(
            src_ref=source, dst_ref=target, send_sem=send_sem, recv_sem=recv_sem,
            device_id={"panel": peer}, device_id_type=pl.DeviceIdType.MESH,
        )

    barrier = pltpu.get_barrier_semaphore()
    for peer in peers:
        pl.semaphore_signal(
            barrier, inc=1, device_id={"panel": peer}, device_id_type=pl.DeviceIdType.MESH
        )
    pl.semaphore_wait(barrier, n - 1)

    arrival = [*range(steps - 2, -1, -1), steps - 1]
    order = [(arrival[k], hop) for k, hop in send_order(steps, n - 1)]
    ring, landed, sent = {}, set(), []

    def land(k, hop):
        if (k, hop) not in landed:
            ring[k, hop].wait_recv()
            landed.add((k, hop))

    def pump(count):
        for _ in range(min(count, len(order) - len(ring))):
            k, hop = order[len(ring)]
            owner = lax.rem(me - hop + n, n)
            if hop > 0:
                land(k, hop - 1)
            source = e_ref.at[k] if hop == 0 else whole_ref.at[k, part(owner)]
            ring[k, hop] = copy(
                source, whole_ref.at[k, part(owner)], e_send.at[k, hop], e_recv.at[k, hop], right
            )
            ring[k, hop].start()

    def complete(k):
        while (k, n - 2) not in ring:
            pump(1)
        land(k, n - 2)

    pump(3)
    for d, peer in enumerate(peers):
        small = copy(g_ref, offsets_ref.at[me], g_send.at[d], g_recv.at[d], peer)
        small.start()
        sent.append(small)
    smalls = list(sent)
    offsets_ref[me] = g_ref[...]
    for k in range(steps):
        whole_ref[k, part(me)] = e_ref[k]
    covs_ref[steps - 1] = l_ref[steps - 1]

    def compose(k):
        @pl.loop(0, width // 128)
        def _(tile):
            at = pl.ds(pl.multiple_of(tile * 128, 128), 128)
            after = whole_ref[steps - 1] if k == steps - 2 else gains[k + 1][...]
            gains[k][at] = three_pass(whole_ref[k, at], after, 0)

    for k in range(steps - 2, -1, -1):
        complete(k)
        if k > 0:
            pump(2)
        columns_ref[k] = three_pass(whole_ref[k], covs_ref[k + 1], 1)
        swaps = []
        for d, peer in enumerate(peers):
            swap = copy(
                columns_ref.at[k, part(peer)], pieces_ref.at[k, me],
                z_send.at[k, d], z_recv.at[k, d], peer,
            )
            swap.start()
            swaps.append(swap)
        pieces_ref[k, me] = columns_ref[k, part(me)]
        if k == 0:
            pump(len(order))
        for swap in swaps:
            swap.wait_recv()
        sent.extend(swaps)
        pieces = jnp.concatenate([pieces_ref[k, p] for p in range(n)], axis=1)
        covs_ref[k] = three_pass(pieces, whole_ref[k], 1) + l_ref[k]

    kept = n // 2 + 1
    later = list(range(steps - 2, -1, -1))
    for j in range(kept):
        at = part(lax.rem(me + j, n))
        cov_ref[part(me), at] = covs_ref[0, :, at]
    for hop in range(n - 1):
        owner = lax.rem(me - hop + n, n)
        moves = []
        for j in range(kept):
            at = part(lax.rem(owner + j, n))
            source = covs_ref.at[0, :, at] if hop == 0 else cov_ref.at[part(owner), at]
            move = copy(
                source, cov_ref.at[part(owner), at], c_send.at[hop, j], c_recv.at[hop, j], right
            )
            move.start()
            moves.append(move)
        if later:
            if hop == 0:
                complete(steps - 1)
            compose(later.pop(0))
        for move in moves:
            move.wait_recv()
        sent.extend(moves)
    for k in later:
        compose(k)
    for small in smalls:
        small.wait_recv()
    for k in range(steps - 1, -1, -1):
        row = jnp.concatenate([offsets_ref[p, k : k + 1] for p in range(n)], axis=1)
        row = jnp.broadcast_to(row, (8, width))
        if k < steps - 1:
            row = three_pass(means_ref[k + 1], whole_ref[k], 1) + row
        means_ref[k] = row
    cov_ref[width : width + 8] = means_ref[0]
    cov_ref[width + 8 :] = jnp.zeros((8, width), jnp.float32)
    for p in range(n):
        for j in range(kept, n):
            q = (p + j) % n
            cov_ref[p * rows : (p + 1) * rows, q * rows : (q + 1) * rows] = cov_ref[
                q * rows : (q + 1) * rows, p * rows : (p + 1) * rows
            ].T
    last_ref[...] = whole_ref[steps - 1]
    own_ref[steps - 1] = e_ref[steps - 1]
    for k in range(steps - 1):
        own_ref[k] = gains[k][part(me)]
    for move in [*ring.values(), *sent]:
        move.wait_send()


def block_element(transitions, offsets, noise_cov):
    steps, rows, width = transitions.shape
    n = lax.axis_size("panel")
    f32 = jnp.float32
    vmem = pl.BlockSpec(memory_space=pltpu.VMEM)
    dma = pltpu.SemaphoreType.DMA
    return pl.pallas_call(
        functools.partial(block_kernel, n),
        out_shape=(
            jax.ShapeDtypeStruct((width, width), f32),
            jax.ShapeDtypeStruct((steps, rows, width), f32),
            jax.ShapeDtypeStruct((steps, rows, width), f32),
            jax.ShapeDtypeStruct((width + 16, width), f32),
            jax.ShapeDtypeStruct((n, steps, rows), f32),
            jax.ShapeDtypeStruct((steps, 8, width), f32),
            *[jax.ShapeDtypeStruct((width, width), f32)] * (steps - 1),
        ),
        in_specs=[vmem] * 3,
        out_specs=(vmem,) * (steps + 5),
        scratch_shapes=[
            pltpu.VMEM((steps, width, width), f32),
            pltpu.VMEM((steps - 1, width, rows), f32),
            pltpu.VMEM((steps - 1, n, rows, rows), f32),
            dma((steps, n - 1)), dma((steps, n - 1)),
            dma((steps - 1, n - 1)), dma((steps - 1, n - 1)),
            dma((n - 1, n // 2 + 1)), dma((n - 1, n // 2 + 1)), dma((n - 1,)), dma((n - 1,)),
        ],
        compiler_params=pltpu.CompilerParams(
            collective_id=0, has_side_effects=True, vmem_limit_bytes=48 * 2**20
        ),
        cost_estimate=pl.CostEstimate(
            flops=18 * width**3, bytes_accessed=12 * 2**20, transcendentals=0
        ),
    )(transitions, offsets, noise_cov)


def scan_kernel(blocks, cov_ref, own_ref, covs_ref, *more):
    steps, rows, width = covs_ref.shape
    gains = more[:steps]
    (out_ref, mean_ref, swap_a, swap_c, first, later_c, g_a, g_c, x_a, x_c, got_a, got_c,
     s_send, s_recv, c_send, c_recv, cw_send, cw_recv, a_send, a_recv, aw_send,
     aw_recv) = more[steps:]
    a_ref = gains[0]
    f32 = jnp.float32
    me = lax.axis_index("tm")
    core = lax.rem(me, 2)
    partner = me + 1 - 2 * core
    tile_rows = 256

    def copy(source, target, send_sem, recv_sem, peer):
        return pltpu.make_async_remote_copy(
            src_ref=source, dst_ref=target, send_sem=send_sem, recv_sem=recv_sem,
            device_id={"tm": peer}, device_id_type=pl.DeviceIdType.MESH,
        )

    def tiles(body):
        @pl.loop(0, width // tile_rows)
        def _(tile):
            body(pl.ds(pl.multiple_of(tile * tile_rows, tile_rows), tile_rows))

    def join(out, gain, cov, add):
        def body(at):
            left = three_pass(gain[at], cov[:width], 0)
            out[at] = three_pass(left, gain[...], 1) + add(at)

        tiles(body)
        tail = pl.ds(width, 8)
        out[tail] = three_pass(cov[tail], gain[...], 1) + add(tail)

    def times(out, left, right):
        def body(at):
            out[at] = three_pass(left[at], right(), 0)

        tiles(body)

    levels = []
    distance = 2
    while distance < blocks:
        levels.append(distance)
        distance *= 2

    def half(ref):
        size = ref.shape[0] // 2
        return ref.at[pl.ds(pl.multiple_of(core * size, 8), size)]

    def place(level):
        return lax.rem(me, 2 * levels[level])

    def holds(level):
        at = place(level)
        return (at >= levels[level]) & (at < levels[level] + 2)

    def lower(level):
        return place(level) < levels[level]

    def inner(level):
        return me < blocks - 2 * levels[level]

    def sends(level, source, target, send_sem, recv_sem):
        d = levels[level]
        return [
            copy(half(source), half(target.at[level]), send_sem.at[level, q],
                 recv_sem.at[level], me - d + 2 * q)
            for q in range(d // 2)
        ]

    def c_sends(level):
        return sends(level, g_c, got_c, c_send, c_recv)

    def a_sends(level):
        return sends(level, g_a, got_a, a_send, a_recv)

    def relay(level, target, send_sem, recv_sem):
        part = half(target.at[level])
        return copy(part, part, send_sem.at[level], recv_sem.at[level], partner)

    def receive(level, target, recv_sem, w_send, w_recv):
        part = half(target.at[level])
        copy(part, part, w_send.at[level], recv_sem.at[level], partner).wait_recv()
        move = relay(level, target, w_send, w_recv)
        move.start()
        move.wait_recv()

    def start_c(level):
        @pl.when(holds(level))
        def _():
            for move in c_sends(level):
                move.start()

    def start_a(level):
        if level < len(levels) - 1:
            @pl.when(holds(level) & inner(level))
            def _():
                for move in a_sends(level):
                    move.start()

    barrier = pltpu.get_barrier_semaphore()
    for d in range(1, blocks):
        pl.semaphore_signal(
            barrier, inc=1, device_id={"tm": lax.rem(me + d, blocks)},
            device_id_type=pl.DeviceIdType.MESH,
        )
    pl.semaphore_wait(barrier, blocks - 1)

    swaps = [
        copy(cov_ref, swap_c, s_send.at[0], s_recv.at[0], partner),
        copy(a_ref, swap_a, s_send.at[1], s_recv.at[1], partner),
    ]
    for move in swaps:
        move.start()
    for move in swaps:
        move.wait_recv()
    early = core == 0
    first[...] = jnp.where(early, a_ref[...], swap_a[...])
    later_c[...] = jnp.where(early, swap_c[...], cov_ref[...])
    g_c[width:] = jnp.zeros((16, width), f32)
    join(g_c, first, later_c, lambda at: jnp.where(early, cov_ref[at], swap_c[at]))
    start_c(0)
    times(g_a, first, lambda: jnp.where(early, swap_a[...], a_ref[...]))
    start_a(0)
    row = lax.broadcasted_iota(jnp.int32, (width, width), 0)
    column = lax.broadcasted_iota(jnp.int32, (width, width), 1)
    x_a[...] = jnp.where(early, swap_a[...], (row == column).astype(f32))
    x_c[...] = jnp.where(early, swap_c[...], 0.0)

    for level in range(len(levels)):
        final = level == len(levels) - 1

        @pl.when(lower(level))
        def _():
            receive(level, got_c, c_recv, cw_send, cw_recv)

        if not final:
            @pl.when(place(level) < 2)
            def _():
                join(g_c, g_a, got_c.at[level], lambda at: g_c[at])

            start_c(level + 1)

        @pl.when(lower(level))
        def _():
            join(x_c, x_a, got_c.at[level], lambda at: x_c[at])

        if not final:
            @pl.when(lower(level) & inner(level))
            def _():
                receive(level, got_a, a_recv, aw_send, aw_recv)
                times(x_a, x_a, lambda: got_a[level])

            @pl.when((place(level) < 2) & inner(level))
            def _():
                times(g_a, g_a, lambda: got_a[level])

            start_a(level + 1)

    for k in range(steps):
        left = three_pass(own_ref[k * rows : (k + 1) * rows], x_c[:width], 0)
        out_ref[k] = three_pass(left, gains[k][...], 1) + covs_ref[k]
    mean_ref[...] = three_pass(x_c[width : width + 8], own_ref[...], 1)

    for move in swaps:
        move.wait_send()
    for level in range(len(levels)):
        @pl.when(holds(level))
        def _():
            for move in c_sends(level):
                move.wait_send()

        @pl.when(lower(level))
        def _():
            relay(level, got_c, cw_send, cw_recv).wait_send()

        if level < len(levels) - 1:
            @pl.when(holds(level) & inner(level))
            def _():
                for move in a_sends(level):
                    move.wait_send()

            @pl.when(lower(level) & inner(level))
            def _():
                relay(level, got_a, aw_send, aw_recv).wait_send()


def scan_and_smooth(cov, own, covs, gains):
    steps, rows, width = covs.shape
    blocks = lax.axis_size("tm")
    f32 = jnp.float32
    vmem = pl.BlockSpec(memory_space=pltpu.VMEM)
    dma = pltpu.SemaphoreType.DMA
    levels = blocks.bit_length() - 2
    square, tall = pltpu.VMEM((width, width), f32), pltpu.VMEM((width + 16, width), f32)
    out, mean = pl.pallas_call(
        functools.partial(scan_kernel, blocks),
        out_shape=(
            jax.ShapeDtypeStruct((steps, rows, width), f32),
            jax.ShapeDtypeStruct((8, steps * rows), f32),
        ),
        in_specs=[vmem] * (3 + steps),
        out_specs=(vmem, vmem),
        scratch_shapes=[
            square, tall, square, tall, square, tall, square, tall,
            pltpu.VMEM((levels, width, width), f32),
            pltpu.VMEM((levels, width + 16, width), f32),
            dma((2,)), dma((2,)), dma((levels, blocks // 4)), dma((levels,)),
            dma((levels,)), dma((levels,)), dma((levels, blocks // 4)), dma((levels,)),
            dma((levels,)), dma((levels,)),
        ],
        compiler_params=pltpu.CompilerParams(
            collective_id=1, has_side_effects=True, vmem_limit_bytes=48 * 2**20
        ),
        cost_estimate=pl.CostEstimate(
            flops=24 * width**3, bytes_accessed=12 * 2**20, transcendentals=0
        ),
    )(cov, own, covs, *gains)
    return mean, out


def send(value, pairs):
    return lax.ppermute(value, "tm", pairs)


def spread(value, core, distance, blocks, groups):
    half = value.shape[0] // 2
    own = jnp.where(core == 0, value[:half], value[half:])
    got = None
    for pair in range(distance // 2):
        pairs = [
            (base + distance + c, base + 2 * pair + c) for base in groups for c in range(2)
        ]
        part = send(own, pairs)
        got = part if got is None else got + part
    other = send(got, [(t, t ^ 1) for t in range(blocks)])
    return jnp.where(
        core == 0, jnp.concatenate([got, other]), jnp.concatenate([other, got])
    )


def later_state(gains, offsets, covs):
    blocks = lax.axis_size("tm")
    me = lax.axis_index("tm")
    core = me % 2
    swap = [(t, t ^ 1) for t in range(blocks)]
    r_gain, r_offset, r_cov = send(gains, swap), send(offsets, swap), send(covs, swap)
    lower = core == 0
    eye = jnp.eye(gains.shape[0], dtype=jnp.float32)
    x_gain = jnp.where(lower, r_gain, eye)
    x_offset = jnp.where(lower, r_offset, 0.0)
    x_cov = jnp.where(lower, r_cov, 0.0)
    first = jnp.where(lower, gains, r_gain)
    g_offset = matvec(first, jnp.where(lower, r_offset, offsets)) + jnp.where(
        lower, offsets, r_offset
    )
    g_cov = product_t(product(first, jnp.where(lower, r_cov, covs)), first) + jnp.where(
        lower, covs, r_cov
    )
    g_gain = product(first, jnp.where(lower, r_gain, gains))
    distance = 2
    while distance < blocks:
        last = 2 * distance == blocks
        groups = list(range(0, blocks, 2 * distance))
        r_cov = spread(g_cov, core, distance, blocks, groups)
        r_offset = spread(g_offset, core, distance, blocks, groups)
        lower = (me // distance) % 2 == 0
        new_cov = product_t(product(x_gain, r_cov), x_gain) + x_cov
        new_offset = matvec(x_gain, r_offset) + x_offset
        if not last:
            r_gain = spread(g_gain, core, distance, blocks, groups[:-1])
            g_offset = matvec(g_gain, r_offset) + g_offset
            g_cov = product_t(product(g_gain, r_cov), g_gain) + g_cov
            g_gain = product(g_gain, r_gain)
            x_gain = jnp.where(lower, product(x_gain, r_gain), x_gain)
        x_cov = jnp.where(lower, new_cov, x_cov)
        x_offset = jnp.where(lower, new_offset, x_offset)
        distance *= 2
    return x_offset, x_cov


def per_device(transitions, offsets, noise_cov):
    steps, rows = transitions.shape[:2]
    start = lax.axis_index("panel") * rows
    if rows % 128 == 0 and steps > 1 and lax.axis_size("tm") > 2:
        last, own, covs, whole_cov, _, means, *composed = block_element(
            transitions, offsets, noise_cov
        )
        gains = [*composed, last]
        mean, out = scan_and_smooth(whole_cov, own.reshape(steps * rows, -1), covs, gains)
        rows_mean = lax.dynamic_slice_in_dim(means[:, 0], start, rows, 1)
        return mean[0].reshape(steps, rows) + rows_mean, out
    else:
        whole = {}
        for k in [*range(steps - 2, -1, -1), steps - 1]:
            whole[k] = lax.all_gather(transitions[k], "panel", axis=0, tiled=True)
        all_offsets = lax.all_gather(offsets, "panel", axis=1, tiled=True)
        cov = noise_cov[steps - 1]
        offset = all_offsets[steps - 1]
        gain = whole[steps - 1]
        covs, gains, means = [cov], [gain], [offset]
        for k in range(steps - 2, -1, -1):
            columns = product_t(whole[k], cov)
            mine = lax.all_to_all(columns, "panel", split_axis=0, concat_axis=1, tiled=True)
            cov = product_t(mine, whole[k]) + noise_cov[k]
            gain = product(whole[k], gain)
            offset = matvec(whole[k], offset) + all_offsets[k]
            covs.append(cov)
            gains.append(gain)
            means.append(offset)
        whole_cov = lax.all_gather(cov, "panel", axis=0, tiled=True)
        own = jnp.concatenate(
            [lax.dynamic_slice_in_dim(f, start, rows, 0) for f in gains[::-1]]
        )
    next_mean, next_cov = later_state(gain, offset, whole_cov)
    covs, gains, means = covs[::-1], gains[::-1], means[::-1]
    own_offsets = jnp.concatenate(
        [lax.dynamic_slice_in_dim(m, start, rows, 0) for m in means]
    )
    mean = (matvec(own, next_mean) + own_offsets).reshape(steps, rows)
    left = product(own, next_cov).reshape(steps, rows, -1)
    out = jnp.stack([product_t(left[k], gains[k]) + covs[k] for k in range(steps)])
    return mean, out


def solution(mesh):
    placed = (P("tm", "panel", None), P("tm", "panel"), P("tm", "panel", None))
    return jax.shard_map(
        per_device,
        mesh=mesh,
        in_specs=placed,
        out_specs=(P("tm", "panel"), P("tm", "panel", None)),
        check_vma=False,
    )
```

```python
import functools

import jax
import jax.numpy as jnp
from jax import lax
from jax.experimental import pallas as pl
from jax.experimental.pallas import tpu as pltpu
from jax.sharding import PartitionSpec as P


def product(left, right):
    return jnp.dot(left, right, precision=lax.Precision.HIGH, preferred_element_type=jnp.float32)


def product_t(left, right):
    return lax.dot_general(
        left, right, (((1,), (1,)), ((), ())),
        precision=lax.Precision.HIGH, preferred_element_type=jnp.float32,
    )


def matvec(matrix, vector):
    return jnp.sum(matrix * vector[None, :], axis=1)


def halves(value):
    high = value.astype(jnp.bfloat16)
    return high, (value - high.astype(jnp.float32)).astype(jnp.bfloat16)


def three_pass(left, right, across):
    dims = (((1,), (across,)), ((), ()))
    left_high, left_low = halves(left)
    right_high, right_low = halves(right)

    def dot(a, b):
        return lax.dot_general(a, b, dims, preferred_element_type=jnp.float32)

    return dot(left_high, right_high) + (dot(left_high, right_low) + dot(left_low, right_high))


def send_order(steps, hops):
    sends = [(k, hop) for hop in range(hops) for k in range(steps)]
    return sorted(sends, key=lambda send: 3 * send[1] + send[0] + 4 * (send[0] // 3))


def block_kernel(
    n, e_ref, g_ref, l_ref, last_ref, own_ref, covs_ref, cov_ref, offsets_ref, means_ref, *more
):
    steps, rows, width = e_ref.shape
    gains = more[: steps - 1]
    (whole_ref, columns_ref, pieces_ref, e_send, e_recv, z_send, z_recv, c_send, c_recv, g_send,
     g_recv) = more[steps - 1 :]
    me = lax.axis_index("panel")
    right = lax.rem(me + 1, n)
    peers = [lax.rem(me + d, n) for d in range(1, n)]

    def part(owner):
        return pl.ds(pl.multiple_of(owner * rows, rows), rows)

    def copy(source, target, send_sem, recv_sem, peer):
        return pltpu.make_async_remote_copy(
            src_ref=source, dst_ref=target, send_sem=send_sem, recv_sem=recv_sem,
            device_id={"panel": peer}, device_id_type=pl.DeviceIdType.MESH,
        )

    barrier = pltpu.get_barrier_semaphore()
    for peer in peers:
        pl.semaphore_signal(
            barrier, inc=1, device_id={"panel": peer}, device_id_type=pl.DeviceIdType.MESH
        )
    pl.semaphore_wait(barrier, n - 1)

    arrival = [*range(steps - 2, -1, -1), steps - 1]
    order = [(arrival[k], hop) for k, hop in send_order(steps, n - 1)]
    ring, landed, sent = {}, set(), []

    def land(k, hop):
        if (k, hop) not in landed:
            ring[k, hop].wait_recv()
            landed.add((k, hop))

    def pump(count):
        for _ in range(min(count, len(order) - len(ring))):
            k, hop = order[len(ring)]
            owner = lax.rem(me - hop + n, n)
            if hop > 0:
                land(k, hop - 1)
            source = e_ref.at[k] if hop == 0 else whole_ref.at[k, part(owner)]
            ring[k, hop] = copy(
                source, whole_ref.at[k, part(owner)], e_send.at[k, hop], e_recv.at[k, hop], right
            )
            ring[k, hop].start()

    def complete(k):
        while (k, n - 2) not in ring:
            pump(1)
        land(k, n - 2)

    pump(3)
    for d, peer in enumerate(peers):
        small = copy(g_ref, offsets_ref.at[me], g_send.at[d], g_recv.at[d], peer)
        small.start()
        sent.append(small)
    smalls = list(sent)
    offsets_ref[me] = g_ref[...]
    for k in range(steps):
        whole_ref[k, part(me)] = e_ref[k]
    covs_ref[steps - 1] = l_ref[steps - 1]

    def compose(k):
        @pl.loop(0, width // 128)
        def _(tile):
            at = pl.ds(pl.multiple_of(tile * 128, 128), 128)
            after = whole_ref[steps - 1] if k == steps - 2 else gains[k + 1][...]
            gains[k][at] = three_pass(whole_ref[k, at], after, 0)

    for k in range(steps - 2, -1, -1):
        complete(k)
        if k > 0:
            pump(2)
        columns_ref[k] = three_pass(whole_ref[k], covs_ref[k + 1], 1)
        swaps = []
        for d, peer in enumerate(peers):
            swap = copy(
                columns_ref.at[k, part(peer)], pieces_ref.at[k, me],
                z_send.at[k, d], z_recv.at[k, d], peer,
            )
            swap.start()
            swaps.append(swap)
        pieces_ref[k, me] = columns_ref[k, part(me)]
        if k == 0:
            pump(len(order))
        for swap in swaps:
            swap.wait_recv()
        sent.extend(swaps)
        pieces = jnp.concatenate([pieces_ref[k, p] for p in range(n)], axis=1)
        covs_ref[k] = three_pass(pieces, whole_ref[k], 1) + l_ref[k]

    kept = n // 2 + 1
    blocks = [part(lax.rem(me + j, n)) for j in range(kept)]
    moves = []
    for d, peer in enumerate(peers):
        for j, at in enumerate(blocks):
            move = copy(
                covs_ref.at[0, :, at], cov_ref.at[part(me), at],
                c_send.at[d, j], c_recv.at[d, j], peer,
            )
            move.start()
            moves.append(move)
    sent.extend(moves)
    for at in blocks:
        cov_ref[part(me), at] = covs_ref[0, :, at]
    for small in smalls:
        small.wait_recv()
    for k in range(steps - 1, -1, -1):
        row = jnp.concatenate([offsets_ref[p, k : k + 1] for p in range(n)], axis=1)
        row = jnp.broadcast_to(row, (8, width))
        if k < steps - 1:
            row = three_pass(means_ref[k + 1], whole_ref[k], 1) + row
        means_ref[k] = row
    cov_ref[width : width + 8] = means_ref[0]
    cov_ref[width + 8 :] = jnp.zeros((8, width), jnp.float32)
    complete(steps - 1)
    for k in range(steps - 2, -1, -1):
        compose(k)
    for move in moves:
        move.wait_recv()
    for p in range(n):
        for j in range(kept, n):
            q = (p + j) % n
            cov_ref[p * rows : (p + 1) * rows, q * rows : (q + 1) * rows] = cov_ref[
                q * rows : (q + 1) * rows, p * rows : (p + 1) * rows
            ].T
    last_ref[...] = whole_ref[steps - 1]
    own_ref[steps - 1] = e_ref[steps - 1]
    for k in range(steps - 1):
        own_ref[k] = gains[k][part(me)]
    for move in [*ring.values(), *sent]:
        move.wait_send()


def block_element(transitions, offsets, noise_cov):
    steps, rows, width = transitions.shape
    n = lax.axis_size("panel")
    f32 = jnp.float32
    vmem = pl.BlockSpec(memory_space=pltpu.VMEM)
    dma = pltpu.SemaphoreType.DMA
    return pl.pallas_call(
        functools.partial(block_kernel, n),
        out_shape=(
            jax.ShapeDtypeStruct((width, width), f32),
            jax.ShapeDtypeStruct((steps, rows, width), f32),
            jax.ShapeDtypeStruct((steps, rows, width), f32),
            jax.ShapeDtypeStruct((width + 16, width), f32),
            jax.ShapeDtypeStruct((n, steps, rows), f32),
            jax.ShapeDtypeStruct((steps, 8, width), f32),
            *[jax.ShapeDtypeStruct((width, width), f32)] * (steps - 1),
        ),
        in_specs=[vmem] * 3,
        out_specs=(vmem,) * (steps + 5),
        scratch_shapes=[
            pltpu.VMEM((steps, width, width), f32),
            pltpu.VMEM((steps - 1, width, rows), f32),
            pltpu.VMEM((steps - 1, n, rows, rows), f32),
            dma((steps, n - 1)), dma((steps, n - 1)),
            dma((steps - 1, n - 1)), dma((steps - 1, n - 1)),
            dma((n - 1, n // 2 + 1)), dma((n - 1, n // 2 + 1)), dma((n - 1,)), dma((n - 1,)),
        ],
        compiler_params=pltpu.CompilerParams(
            collective_id=0, has_side_effects=True, vmem_limit_bytes=48 * 2**20
        ),
        cost_estimate=pl.CostEstimate(
            flops=18 * width**3, bytes_accessed=12 * 2**20, transcendentals=0
        ),
    )(transitions, offsets, noise_cov)


def scan_kernel(blocks, cov_ref, own_ref, covs_ref, *more):
    steps, rows, width = covs_ref.shape
    gains = more[:steps]
    (out_ref, mean_ref, swap_a, swap_c, first, later_c, g_a, g_c, x_a, x_c, got_a, got_c,
     s_send, s_recv, c_send, c_recv, cw_send, cw_recv, a_send, a_recv, aw_send,
     aw_recv) = more[steps:]
    a_ref = gains[0]
    f32 = jnp.float32
    me = lax.axis_index("tm")
    core = lax.rem(me, 2)
    partner = me + 1 - 2 * core
    tile_rows = 256

    def copy(source, target, send_sem, recv_sem, peer):
        return pltpu.make_async_remote_copy(
            src_ref=source, dst_ref=target, send_sem=send_sem, recv_sem=recv_sem,
            device_id={"tm": peer}, device_id_type=pl.DeviceIdType.MESH,
        )

    def tiles(body):
        @pl.loop(0, width // tile_rows)
        def _(tile):
            body(pl.ds(pl.multiple_of(tile * tile_rows, tile_rows), tile_rows))

    def join(out, gain, cov, add):
        def body(at):
            left = three_pass(gain[at], cov[:width], 0)
            out[at] = three_pass(left, gain[...], 1) + add(at)

        tiles(body)
        tail = pl.ds(width, 8)
        out[tail] = three_pass(cov[tail], gain[...], 1) + add(tail)

    def times(out, left, right):
        def body(at):
            out[at] = three_pass(left[at], right(), 0)

        tiles(body)

    levels = []
    distance = 2
    while distance < blocks:
        levels.append(distance)
        distance *= 2

    def half(ref):
        size = ref.shape[0] // 2
        return ref.at[pl.ds(pl.multiple_of(core * size, 8), size)]

    def place(level):
        return lax.rem(me, 2 * levels[level])

    def holds(level):
        at = place(level)
        return (at >= levels[level]) & (at < levels[level] + 2)

    def lower(level):
        return place(level) < levels[level]

    def inner(level):
        return me < blocks - 2 * levels[level]

    def sends(level, source, target, send_sem, recv_sem):
        d = levels[level]
        return [
            copy(half(source), half(target.at[level]), send_sem.at[level, q],
                 recv_sem.at[level], me - d + 2 * q)
            for q in range(d // 2)
        ]

    def c_sends(level):
        return sends(level, g_c, got_c, c_send, c_recv)

    def a_sends(level):
        return sends(level, g_a, got_a, a_send, a_recv)

    def relay(level, target, send_sem, recv_sem):
        part = half(target.at[level])
        return copy(part, part, send_sem.at[level], recv_sem.at[level], partner)

    def receive(level, target, recv_sem, w_send, w_recv):
        part = half(target.at[level])
        copy(part, part, w_send.at[level], recv_sem.at[level], partner).wait_recv()
        move = relay(level, target, w_send, w_recv)
        move.start()
        move.wait_recv()

    def start_c(level):
        @pl.when(holds(level))
        def _():
            for move in c_sends(level):
                move.start()

    def start_a(level):
        if level < len(levels) - 1:
            @pl.when(holds(level) & inner(level))
            def _():
                for move in a_sends(level):
                    move.start()

    barrier = pltpu.get_barrier_semaphore()
    for d in range(1, blocks):
        pl.semaphore_signal(
            barrier, inc=1, device_id={"tm": lax.rem(me + d, blocks)},
            device_id_type=pl.DeviceIdType.MESH,
        )
    pl.semaphore_wait(barrier, blocks - 1)

    swaps = [
        copy(cov_ref, swap_c, s_send.at[0], s_recv.at[0], partner),
        copy(a_ref, swap_a, s_send.at[1], s_recv.at[1], partner),
    ]
    for move in swaps:
        move.start()
    for move in swaps:
        move.wait_recv()
    early = core == 0
    first[...] = jnp.where(early, a_ref[...], swap_a[...])
    later_c[...] = jnp.where(early, swap_c[...], cov_ref[...])
    g_c[width:] = jnp.zeros((16, width), f32)
    join(g_c, first, later_c, lambda at: jnp.where(early, cov_ref[at], swap_c[at]))
    start_c(0)
    times(g_a, first, lambda: jnp.where(early, swap_a[...], a_ref[...]))
    start_a(0)
    row = lax.broadcasted_iota(jnp.int32, (width, width), 0)
    column = lax.broadcasted_iota(jnp.int32, (width, width), 1)
    x_a[...] = jnp.where(early, swap_a[...], (row == column).astype(f32))
    x_c[...] = jnp.where(early, swap_c[...], 0.0)

    for level in range(len(levels)):
        final = level == len(levels) - 1

        @pl.when(lower(level))
        def _():
            receive(level, got_c, c_recv, cw_send, cw_recv)

        if not final:
            @pl.when(place(level) < 2)
            def _():
                join(g_c, g_a, got_c.at[level], lambda at: g_c[at])

            start_c(level + 1)

        @pl.when(lower(level))
        def _():
            join(x_c, x_a, got_c.at[level], lambda at: x_c[at])

        if not final:
            @pl.when(lower(level) & inner(level))
            def _():
                receive(level, got_a, a_recv, aw_send, aw_recv)
                times(x_a, x_a, lambda: got_a[level])

            @pl.when((place(level) < 2) & inner(level))
            def _():
                times(g_a, g_a, lambda: got_a[level])

            start_a(level + 1)

    for k in range(steps):
        left = three_pass(own_ref[k * rows : (k + 1) * rows], x_c[:width], 0)
        out_ref[k] = three_pass(left, gains[k][...], 1) + covs_ref[k]
    mean_ref[...] = three_pass(x_c[width : width + 8], own_ref[...], 1)

    for move in swaps:
        move.wait_send()
    for level in range(len(levels)):
        @pl.when(holds(level))
        def _():
            for move in c_sends(level):
                move.wait_send()

        @pl.when(lower(level))
        def _():
            relay(level, got_c, cw_send, cw_recv).wait_send()

        if level < len(levels) - 1:
            @pl.when(holds(level) & inner(level))
            def _():
                for move in a_sends(level):
                    move.wait_send()

            @pl.when(lower(level) & inner(level))
            def _():
                relay(level, got_a, aw_send, aw_recv).wait_send()


def scan_and_smooth(cov, own, covs, gains):
    steps, rows, width = covs.shape
    blocks = lax.axis_size("tm")
    f32 = jnp.float32
    vmem = pl.BlockSpec(memory_space=pltpu.VMEM)
    dma = pltpu.SemaphoreType.DMA
    levels = blocks.bit_length() - 2
    square, tall = pltpu.VMEM((width, width), f32), pltpu.VMEM((width + 16, width), f32)
    out, mean = pl.pallas_call(
        functools.partial(scan_kernel, blocks),
        out_shape=(
            jax.ShapeDtypeStruct((steps, rows, width), f32),
            jax.ShapeDtypeStruct((8, steps * rows), f32),
        ),
        in_specs=[vmem] * (3 + steps),
        out_specs=(vmem, vmem),
        scratch_shapes=[
            square, tall, square, tall, square, tall, square, tall,
            pltpu.VMEM((levels, width, width), f32),
            pltpu.VMEM((levels, width + 16, width), f32),
            dma((2,)), dma((2,)), dma((levels, blocks // 4)), dma((levels,)),
            dma((levels,)), dma((levels,)), dma((levels, blocks // 4)), dma((levels,)),
            dma((levels,)), dma((levels,)),
        ],
        compiler_params=pltpu.CompilerParams(
            collective_id=1, has_side_effects=True, vmem_limit_bytes=48 * 2**20
        ),
        cost_estimate=pl.CostEstimate(
            flops=24 * width**3, bytes_accessed=12 * 2**20, transcendentals=0
        ),
    )(cov, own, covs, *gains)
    return mean, out


def send(value, pairs):
    return lax.ppermute(value, "tm", pairs)


def spread(value, core, distance, blocks, groups):
    half = value.shape[0] // 2
    own = jnp.where(core == 0, value[:half], value[half:])
    got = None
    for pair in range(distance // 2):
        pairs = [
            (base + distance + c, base + 2 * pair + c) for base in groups for c in range(2)
        ]
        part = send(own, pairs)
        got = part if got is None else got + part
    other = send(got, [(t, t ^ 1) for t in range(blocks)])
    return jnp.where(
        core == 0, jnp.concatenate([got, other]), jnp.concatenate([other, got])
    )


def later_state(gains, offsets, covs):
    blocks = lax.axis_size("tm")
    me = lax.axis_index("tm")
    core = me % 2
    swap = [(t, t ^ 1) for t in range(blocks)]
    r_gain, r_offset, r_cov = send(gains, swap), send(offsets, swap), send(covs, swap)
    lower = core == 0
    eye = jnp.eye(gains.shape[0], dtype=jnp.float32)
    x_gain = jnp.where(lower, r_gain, eye)
    x_offset = jnp.where(lower, r_offset, 0.0)
    x_cov = jnp.where(lower, r_cov, 0.0)
    first = jnp.where(lower, gains, r_gain)
    g_offset = matvec(first, jnp.where(lower, r_offset, offsets)) + jnp.where(
        lower, offsets, r_offset
    )
    g_cov = product_t(product(first, jnp.where(lower, r_cov, covs)), first) + jnp.where(
        lower, covs, r_cov
    )
    g_gain = product(first, jnp.where(lower, r_gain, gains))
    distance = 2
    while distance < blocks:
        last = 2 * distance == blocks
        groups = list(range(0, blocks, 2 * distance))
        r_cov = spread(g_cov, core, distance, blocks, groups)
        r_offset = spread(g_offset, core, distance, blocks, groups)
        lower = (me // distance) % 2 == 0
        new_cov = product_t(product(x_gain, r_cov), x_gain) + x_cov
        new_offset = matvec(x_gain, r_offset) + x_offset
        if not last:
            r_gain = spread(g_gain, core, distance, blocks, groups[:-1])
            g_offset = matvec(g_gain, r_offset) + g_offset
            g_cov = product_t(product(g_gain, r_cov), g_gain) + g_cov
            g_gain = product(g_gain, r_gain)
            x_gain = jnp.where(lower, product(x_gain, r_gain), x_gain)
        x_cov = jnp.where(lower, new_cov, x_cov)
        x_offset = jnp.where(lower, new_offset, x_offset)
        distance *= 2
    return x_offset, x_cov


def per_device(transitions, offsets, noise_cov):
    steps, rows = transitions.shape[:2]
    start = lax.axis_index("panel") * rows
    if rows % 128 == 0 and steps > 1 and lax.axis_size("tm") > 2:
        last, own, covs, whole_cov, _, means, *composed = block_element(
            transitions, offsets, noise_cov
        )
        gains = [*composed, last]
        mean, out = scan_and_smooth(whole_cov, own.reshape(steps * rows, -1), covs, gains)
        rows_mean = lax.dynamic_slice_in_dim(means[:, 0], start, rows, 1)
        return mean[0].reshape(steps, rows) + rows_mean, out
    else:
        whole = {}
        for k in [*range(steps - 2, -1, -1), steps - 1]:
            whole[k] = lax.all_gather(transitions[k], "panel", axis=0, tiled=True)
        all_offsets = lax.all_gather(offsets, "panel", axis=1, tiled=True)
        cov = noise_cov[steps - 1]
        offset = all_offsets[steps - 1]
        gain = whole[steps - 1]
        covs, gains, means = [cov], [gain], [offset]
        for k in range(steps - 2, -1, -1):
            columns = product_t(whole[k], cov)
            mine = lax.all_to_all(columns, "panel", split_axis=0, concat_axis=1, tiled=True)
            cov = product_t(mine, whole[k]) + noise_cov[k]
            gain = product(whole[k], gain)
            offset = matvec(whole[k], offset) + all_offsets[k]
            covs.append(cov)
            gains.append(gain)
            means.append(offset)
        whole_cov = lax.all_gather(cov, "panel", axis=0, tiled=True)
        own = jnp.concatenate(
            [lax.dynamic_slice_in_dim(f, start, rows, 0) for f in gains[::-1]]
        )
    next_mean, next_cov = later_state(gain, offset, whole_cov)
    covs, gains, means = covs[::-1], gains[::-1], means[::-1]
    own_offsets = jnp.concatenate(
        [lax.dynamic_slice_in_dim(m, start, rows, 0) for m in means]
    )
    mean = (matvec(own, next_mean) + own_offsets).reshape(steps, rows)
    left = product(own, next_cov).reshape(steps, rows, -1)
    out = jnp.stack([product_t(left[k], gains[k]) + covs[k] for k in range(steps)])
    return mean, out


def solution(mesh):
    placed = (P("tm", "panel", None), P("tm", "panel"), P("tm", "panel", None))
    return jax.shard_map(
        per_device,
        mesh=mesh,
        in_specs=placed,
        out_specs=(P("tm", "panel"), P("tm", "panel", None)),
        check_vma=False,
    )
```
